256 devices in a mesh: field: 4 (over y_hi, core), tile: 64 (over y_lo, x, z).
Axes of the slice: x: 4, y: 4 (y_hi: 2, y_lo: 2; y = y_hi * 2 + y_lo), z: 8, core: 2. Of those that a mesh axis runs over, the one named last changes fastest.
Arguments:
- density: float32 [64, 4, 8, 128], P('tile'), may hold values from 0.8 to 1.2
- velocity: float32 [3, 64, 4, 8, 128], P(None, 'tile'), may hold values from -3 to 3
- energy: float32 [64, 4, 8, 128], P('tile'), may hold values from 0.8 to 1.2
- species: float32 [16, 16, 64, 4, 8, 128], P('field', None, 'tile'), may hold values from 0 to 1
- wiener: float32 [2, 16, 3, 64, 4, 8, 128], P(None, 'field', None, 'tile'), may hold values from -6 to 6
- substeps: int32 [64, 4, 8, 128], P('tile'), may hold values from 1 to 4
- mix_rate: float32 [64, 4, 8, 128], P('tile'), may hold values from 0.5 to 5
- reactants: float32 [96, 16], replicated, may hold values from -1.5 to 1.5
- stoich: float32 [16, 96], replicated, may hold values from -0.625 to 0.625
- kinetic_constants: float32 [96], replicated, may hold values from 0.2 to 2
- excitation_sensitivity: float32 [96], replicated, may hold values from 0.5 to 4
- heat: float32 [16], replicated, may hold values from -4 to 4
- molar: float32 [16], replicated, may hold values from 0.05 to 0.2
Outputs:
- flow_out: float32 [5, 64, 4, 8, 128], P(None, 'tile')
- species_out: float32 [16, 16, 64, 4, 8, 128], P('field', None, 'tile')
The draws below stay inside these ranges and needn't reach their ends.
All inputs are finite; a program needn't handle non-finite values.
Results may differ from the reference program's by a relative error of at most 0.0003.
Values sent between devices are 32-bit elements; how exact they have to be, the bound alone decides.
No kernel may reach another device: no remote copies, remote signals or barrier semaphores. Data moves between devices by JAX's collectives and lax.ppermute only.
A program may use at most 64 MiB of HBM per device.

```python
import math
import jax
import jax.numpy as jnp
from jax import lax

SPECIES = 16
REACT = 96
REALIZATIONS = 16
SUBS = 4
STEPS = 2
CZ = 4
CY = 8
NX = 128
TILES = 64
TY = 64
N_TILE = 64


def touch_ends(result, rng, smallest, largest):
    shape = result.shape
    spot = [jax.random.randint(jax.random.fold_in(rng, axis), (), 0, shape[axis]) for axis in range(len(shape))]
    result = result.at[tuple(spot)].set(smallest)
    longest = shape.index(max(shape))
    spot[longest] = (spot[longest] + 1) % shape[longest]
    return result.at[tuple(spot)].set(largest)


def block_scale(rng, extent, cuts, least, top_value):
    def one(axis_at, shards_of):
        steps = jax.random.uniform(jax.random.fold_in(jax.random.fold_in(rng, 6), axis_at), (shards_of,), jnp.float32, least / len(cuts), top_value / len(cuts))
        return jnp.repeat(jnp.exp(steps), extent[axis_at] // shards_of).reshape((-1,) + (1,) * (len(extent) - axis_at - 1))

    gain = one(*cuts[0])
    for cut in cuts[1:]:
        gain = gain * one(*cut)
    return gain


def scatter_about(key, shape, width, limit, cuts=(), dtype=jnp.bfloat16):
    loudness = block_scale(key, shape, cuts, -0.22, 0.18) if cuts else 1.0
    entries = jax.random.normal(key, shape, jnp.float32) * width * loudness
    return jnp.minimum(jnp.maximum(entries, -limit), limit).astype(dtype)


def setup_inputs(seed: int = 0) -> dict:
    key_of = jax.random.split(jax.random.key(seed), 14)
    density = jnp.clip(0.8 + 0.40000004 * jax.random.uniform(key_of[0], (TILES, CZ, CY, NX), jnp.float32) ** block_scale(key_of[0], (TILES, CZ, CY, NX), ((0, 64),), -0.2, 0.2), 0.8, 1.2)
    velocity = scatter_about(key_of[1], (3, TILES, CZ, CY, NX), 0.5, 3.0, ((1, 64),), jnp.float32)
    energy = jnp.clip(0.8 + 0.40000004 * jax.random.uniform(key_of[2], (TILES, CZ, CY, NX), jnp.float32) ** block_scale(key_of[2], (TILES, CZ, CY, NX), ((0, 64),), -0.2, 0.2), 0.8, 1.2)
    species = jnp.clip(1.0 * jax.random.uniform(key_of[3], (REALIZATIONS, SPECIES, TILES, CZ, CY, NX), jnp.float32) ** block_scale(key_of[3], (REALIZATIONS, SPECIES, TILES, CZ, CY, NX), ((0, 4), (2, 64)), -0.2, 0.2), 0.0, 1.0)
    wiener = scatter_about(key_of[4], (STEPS, REALIZATIONS, 3, TILES, CZ, CY, NX), 1.0, 6.0, ((1, 4), (3, 64)), jnp.float32)
    substeps = touch_ends(jax.random.randint(key_of[5], (TILES, CZ, CY, NX), 1, SUBS + 1), jax.random.fold_in(key_of[5], 1), 1, SUBS).astype(jnp.int32)
    mix_rate = jnp.clip(jnp.exp(math.log(5.0) - 2.3025851 * jax.random.uniform(key_of[6], (TILES, CZ, CY, NX), jnp.float32) ** block_scale(key_of[6], (TILES, CZ, CY, NX), ((0, 64),), -0.2, 0.2)), 0.5, 5.0)
    reactants = scatter_about(key_of[7], (REACT, SPECIES), SPECIES ** -0.5, 1.5, (), jnp.float32)
    stoich = scatter_about(key_of[8], (SPECIES, REACT), REACT ** -0.5, 0.625, (), jnp.float32)
    kinetic_constants = jnp.clip(jnp.exp(jax.random.uniform(key_of[9], (REACT,), jnp.float32, math.log(0.2), math.log(2.0))), 0.2, 2.0)
    excitation_sensitivity = jnp.clip(jnp.exp(jax.random.uniform(key_of[10], (REACT,), jnp.float32, math.log(0.5), math.log(4.0))), 0.5, 4.0)
    heat = scatter_about(key_of[11], (SPECIES,), 1.0, 4.0, (), jnp.float32)
    molar = jnp.clip(jax.random.uniform(key_of[12], (SPECIES,), jnp.float32, 0.05, 0.2), 0.05, 0.2)
    return {"density": density, "velocity": velocity, "energy": energy, "species": species, "wiener": wiener, "substeps": substeps, "mix_rate": mix_rate, "reactants": reactants, "stoich": stoich, "kinetic_constants": kinetic_constants, "excitation_sensitivity": excitation_sensitivity, "heat": heat, "molar": molar}


time_step = 0.1
viscosity = 0.4
diffusivity = 0.3
relaxation = 2.0
noise_scale = math.sqrt(2.0 * 0.3 * 0.1)

def to_grid(blocks):
    leading = blocks.shape[:-4]
    split = blocks.reshape(leading + (N_TILE // TY, TY, CZ, CY, NX))
    return jnp.swapaxes(split, -4, -3).reshape(leading + (N_TILE // TY * CZ, TY * CY, NX))

def to_blocks(grid):
    leading = grid.shape[:-3]
    split = grid.reshape(leading + (N_TILE // TY, CZ, TY, CY, NX))
    return jnp.swapaxes(split, -4, -3).reshape(leading + (N_TILE, CZ, CY, NX))

def pad_cells(values):
    widths = [(0, 0)] * (values.ndim - 3) + [(1, 1)] * 3
    return jnp.pad(values, widths)

def neighbours(padded):
    centre = padded[..., 1:-1, 1:-1, 1:-1]
    grad_z = (padded[..., 2:, 1:-1, 1:-1] - padded[..., :-2, 1:-1, 1:-1]) * 0.5
    grad_y = (padded[..., 1:-1, 2:, 1:-1] - padded[..., 1:-1, :-2, 1:-1]) * 0.5
    grad_x = (padded[..., 1:-1, 1:-1, 2:] - padded[..., 1:-1, 1:-1, :-2]) * 0.5
    laplacian = padded[..., 2:, 1:-1, 1:-1] + padded[..., :-2, 1:-1, 1:-1]
    laplacian = laplacian + padded[..., 1:-1, 2:, 1:-1] + padded[..., 1:-1, :-2, 1:-1]
    laplacian = laplacian + padded[..., 1:-1, 1:-1, 2:] + padded[..., 1:-1, 1:-1, :-2] - 6.0 * centre
    return (centre, (grad_z, grad_y, grad_x), laplacian)

def flow_update(padded):
    centre, gradients, laplacian = neighbours(padded)
    carried = centre[1] * gradients[0] + centre[2] * gradients[1] + centre[3] * gradients[2]
    return centre + time_step * (viscosity * laplacian - carried)

def march_forward(padded, speeds, noise_draw):
    centre, gradients, laplacian = neighbours(padded)
    carried = speeds[0] * gradients[0] + speeds[1] * gradients[1] + speeds[2] * gradients[2]
    noisy = gradients[0] * noise_draw[:, 0][:, None] + gradients[1] * noise_draw[:, 1][:, None] + gradients[2] * noise_draw[:, 2][:, None]
    return centre + time_step * (diffusivity * laplacian - carried) + noise_scale * noisy

def react_field(flattened, kinetic_multiplier, sub_counts, step_len, reactants, stoich):
    for fractional_increment in range(SUBS):
        driving = jnp.dot(reactants, flattened, precision=lax.Precision.HIGHEST)
        changes = jnp.dot(stoich, kinetic_multiplier * driving, precision=lax.Precision.HIGHEST)
        flattened = flattened + jnp.where(sub_counts > fractional_increment, step_len, 0.0) * changes
    return flattened

def reference(density, velocity, energy, species, wiener, substeps, mix_rate, reactants, stoich, kinetic_constants, excitation_sensitivity, heat, molar):
    fluid_state = jnp.concatenate([to_grid(density)[None], to_grid(velocity), to_grid(energy)[None]], 0)
    species = to_grid(species)
    noise_all = to_grid(wiener)
    mix_grid = to_grid(mix_rate)
    sub_counts = to_grid(substeps).reshape(-1)
    step_len = time_step / sub_counts.astype(jnp.float32)
    number_of_cells = sub_counts.shape[0]
    for current_step_index in range(STEPS):
        fluid_state = flow_update(pad_cells(fluid_state))
        carried = march_forward(pad_cells(species), fluid_state[1:4], noise_all[current_step_index])
        field_mean = lax.optimization_barrier(jnp.sum(carried, 0)) / REALIZATIONS
        mixed = carried - time_step * mix_grid * (carried - field_mean)
        pointwise_thermal_level = fluid_state[4].reshape(-1)
        kinetic_multiplier = kinetic_constants[:, None] * jnp.exp(excitation_sensitivity[:, None] * (pointwise_thermal_level - 1.0))
        flattened = mixed.reshape(REALIZATIONS, SPECIES, number_of_cells)
        reacted = lax.map(lambda one: react_field(one, kinetic_multiplier, sub_counts, step_len, reactants, stoich), flattened)
        heat_released = lax.optimization_barrier(jnp.sum(heat[None, :, None] * (reacted - flattened), (0, 1))) / REALIZATIONS
        density_mean = lax.optimization_barrier(jnp.sum(molar[None, :, None] * reacted, (0, 1))) / REALIZATIONS
        species = reacted.reshape(species.shape)
        heat_released = heat_released.reshape(fluid_state.shape[1:])
        density_mean = density_mean.reshape(fluid_state.shape[1:])
        fluid_state = jnp.concatenate([(fluid_state[0] + time_step * relaxation * (density_mean - fluid_state[0]))[None], fluid_state[1:4], (fluid_state[4] + heat_released)[None]], 0)
    return (to_blocks(fluid_state), to_blocks(species))
```

```python
import math

import jax
import jax.numpy as jnp
from jax import lax
from jax.sharding import PartitionSpec as P

SPECIES = 16
REALIZATIONS = 16
SUBS = 4
STEPS = 2


time_step = 0.1
viscosity = 0.4
diffusivity = 0.3
relaxation = 2.0
noise_scale = math.sqrt(2.0 * 0.3 * 0.1)


def from_behind(value, axis, steps):
    count = lax.axis_size(axis)
    initial, last = (max(0, -steps), min(count, count - steps))
    return lax.ppermute(value, axis, [(source, source + steps) for source in range(initial, last)])


def field_total(value):
    half = value.shape[0] // 2
    core = lax.axis_index("field") % 2
    core_pairs = [(i, i ^ 1) for i in range(4)]
    chip_pairs = [(i, i ^ 2) for i in range(4)]
    mine = jnp.where(core == 0, value[:half], value[half:])
    other = jnp.where(core == 0, value[half:], value[:half])
    mine = mine + lax.ppermute(other, "field", core_pairs)
    mine = mine + lax.ppermute(mine, "field", chip_pairs)
    other = lax.ppermute(mine, "field", core_pairs)
    return jnp.concatenate([jnp.where(core == 0, mine, other), jnp.where(core == 0, other, mine)])


def neighbours(padded):
    centre = padded[..., 1:-1, 1:-1, 1:-1]
    grad_z = (padded[..., 2:, 1:-1, 1:-1] - padded[..., :-2, 1:-1, 1:-1]) * 0.5
    grad_y = (padded[..., 1:-1, 2:, 1:-1] - padded[..., 1:-1, :-2, 1:-1]) * 0.5
    grad_x = (padded[..., 1:-1, 1:-1, 2:] - padded[..., 1:-1, 1:-1, :-2]) * 0.5
    laplacian = padded[..., 2:, 1:-1, 1:-1] + padded[..., :-2, 1:-1, 1:-1]
    laplacian = laplacian + padded[..., 1:-1, 2:, 1:-1] + padded[..., 1:-1, :-2, 1:-1]
    laplacian = (
        laplacian + padded[..., 1:-1, 1:-1, 2:] + padded[..., 1:-1, 1:-1, :-2] - 6.0 * centre
    )
    return (centre, (grad_z, grad_y, grad_x), laplacian)


def flow_update(padded):
    centre, gradients, laplacian = neighbours(padded)
    carried = centre[1] * gradients[0] + centre[2] * gradients[1] + centre[3] * gradients[2]
    return centre + time_step * (viscosity * laplacian - carried)


def march_forward(padded, speeds, noise_draw):
    centre, gradients, laplacian = neighbours(padded)
    carried = speeds[0] * gradients[0] + speeds[1] * gradients[1] + speeds[2] * gradients[2]
    noisy = (
        gradients[0] * noise_draw[:, 0][:, None]
        + gradients[1] * noise_draw[:, 1][:, None]
        + gradients[2] * noise_draw[:, 2][:, None]
    )
    return centre + time_step * (diffusivity * laplacian - carried) + noise_scale * noisy


def react_field(flattened, kinetic_multiplier, sub_counts, step_len, reactants, stoich):
    for fractional_increment in range(SUBS):
        driving = jnp.dot(reactants, flattened, precision=lax.Precision.HIGHEST)
        changes = jnp.dot(stoich, kinetic_multiplier * driving, precision=lax.Precision.HIGHEST)
        flattened = (
            flattened + jnp.where(sub_counts > fractional_increment, step_len, 0.0) * changes
        )
    return flattened


def attach_faces(values, below_y, above_y):
    leading = [(0, 0)] * (values.ndim - 3)
    widened_grid = jnp.concatenate([below_y, values, above_y], values.ndim - 2)
    return jnp.pad(widened_grid, leading + [(1, 1), (0, 0), (1, 1)])


def exchange_faces(fluid_state, scalars):
    below_y = from_behind((fluid_state[:, :, -1:], scalars[:, :, :, -1:]), "tile", 1)
    above_y = from_behind((fluid_state[:, :, :1], scalars[:, :, :, :1]), "tile", -1)
    padded_flow = attach_faces(fluid_state, below_y[0], above_y[0])
    padded_species = attach_faces(scalars, below_y[1], above_y[1])
    return (padded_flow, padded_species)


def on_device(
    density,
    velocity,
    energy,
    species,
    wiener,
    substeps,
    mix_rate,
    reactants,
    stoich,
    kinetic_constants,
    excitation_sensitivity,
    heat,
    molar,
):
    fluid_state = jnp.concatenate([density, velocity[:, 0], energy], 0)
    scalars = species[:, :, 0]
    noise_all = wiener[:, :, :, 0]
    rates = mix_rate[0]
    sub_counts = substeps.reshape(-1)
    step_len = time_step / sub_counts.astype(jnp.float32)
    number_of_cells = sub_counts.shape[0]
    local_fields = scalars.shape[0]
    for current_step_index in range(STEPS):
        padded_flow, padded_species = exchange_faces(fluid_state, scalars)
        fluid_state = flow_update(padded_flow)
        speeds = fluid_state[1:4]
        noise_draw = noise_all[current_step_index]
        carried = march_forward(padded_species, speeds, noise_draw)
        field_sum = field_total(jnp.sum(carried, 0))
        field_mean = field_sum / REALIZATIONS
        mixed = carried - time_step * rates * (carried - field_mean)
        pointwise_thermal_level = fluid_state[4].reshape(-1)
        kinetic_multiplier = kinetic_constants[:, None] * jnp.exp(
            excitation_sensitivity[:, None] * (pointwise_thermal_level - 1.0)
        )
        flattened = mixed.reshape(local_fields, SPECIES, number_of_cells)
        reacted = lax.map(
            lambda one: react_field(
                one, kinetic_multiplier, sub_counts, step_len, reactants, stoich
            ),
            flattened,
        )
        heat_released = jnp.sum(heat[None, :, None] * (reacted - flattened), (0, 1))
        density_sum = jnp.sum(molar[None, :, None] * reacted, (0, 1))
        scalars = reacted.reshape(scalars.shape)
        partials = jnp.stack([density_sum, heat_released], 0).reshape((2,) + fluid_state.shape[1:])
        returned = field_total(partials) / REALIZATIONS
        fluid_state = jnp.concatenate(
            [
                (fluid_state[0] + time_step * relaxation * (returned[0] - fluid_state[0]))[None],
                fluid_state[1:4],
                (fluid_state[4] + returned[1])[None],
            ],
            0,
        )
    return (fluid_state[:, None], scalars[:, :, None])


def solution(mesh):
    placed = (
        P("tile", None, None, None),
        P(None, "tile", None, None, None),
        P("tile", None, None, None),
        P("field", None, "tile", None, None, None),
        P(None, "field", None, "tile", None, None, None),
        P("tile", None, None, None),
        P("tile", None, None, None),
        P(),
        P(),
        P(),
        P(),
        P(),
        P(),
    )
    return jax.shard_map(
        on_device,
        mesh=mesh,
        in_specs=placed,
        out_specs=(P(None, "tile", None, None, None), P("field", None, "tile", None, None, None)),
        check_vma=False,
    )
```

```python
import math

import jax
import jax.numpy as jnp
from jax import lax
from jax.experimental import pallas as pl
from jax.experimental.pallas import tpu as pltpu
from jax.sharding import PartitionSpec as P

FIELDS = 4
SPECIES = 16
ALL_FIELDS = 16
REACT = 96
SUBS = 4
CZ, CY, NX = 4, 8, 128

time_step = 0.1
viscosity = 0.4
diffusivity = 0.3
relaxation = 2.0
noise_half = 0.5 * math.sqrt(2.0 * 0.3 * 0.1)
speed_half = 0.5 * time_step
spread = time_step * diffusivity
f32 = jnp.float32
bf16 = jnp.bfloat16

SPECIES_ROWS = 2 * FIELDS * CZ * SPECIES
FLOW_ROWS = 2 * CZ * 8
MESSAGE_ROWS = SPECIES_ROWS + FLOW_ROWS + CZ * 16


def lanes(shape):
    return lax.broadcasted_iota(jnp.int32, shape, 1)


def shift_x(value, lane):
    ahead = jnp.where(lane == NX - 1, 0.0, pltpu.roll(value, NX - 1, 1))
    behind = jnp.where(lane == 0, 0.0, pltpu.roll(value, 1, 1))
    return ahead, behind


def stencil(column, above, below, z, lane):
    zero = jnp.zeros_like(column[z])
    up = column[z + 1] if z + 1 < CZ else zero
    down = column[z - 1] if z > 0 else zero
    ahead, behind = shift_x(column[z], lane)
    total = (up + down) + (above[z] + below[z]) + (ahead + behind)
    return total, (up - down, above[z] - below[z], ahead - behind)


def pack(
    species, density, velocity, energy, wiener, mix, substeps,
    low, high, own, flow, noise_first, noise_second,
):
    for z in range(CZ):
        base = z * CY * 8
        rows = [density[0, z], velocity[0, 0, z], velocity[1, 0, z], velocity[2, 0, z], energy[0, z],
                time_step * mix[0, z], substeps[0, z].astype(f32), jnp.zeros((CY, NX), f32)]
        for v in range(8):
            for y in range(CY):
                flow[y, z, v : v + 1] = rows[v][y : y + 1]

    def layer(y, _):
        for z in range(CZ):
            for f in range(FIELDS):
                own[y, f, z] = species[pl.ds(f * 512 + z * 8 + y, SPECIES, stride=32), :]
            noise_first[y, z] = jnp.concatenate(
                [wiener[pl.ds(z * 8 + y, 12, stride=32), :], jnp.zeros((4, NX), f32)], 0
            )
            noise_second[y, z] = jnp.concatenate(
                [wiener[pl.ds(384 + z * 8 + y, 12, stride=32), :], jnp.zeros((4, NX), f32)], 0
            )
        return 0

    lax.fori_loop(0, CY, layer, 0)
    for out, first, edge in ((low, 0, 0), (high, CY - 2, CY - 1)):
        for y in range(2):
            for f in range(FIELDS):
                for z in range(CZ):
                    row = ((y * FIELDS + f) * CZ + z) * SPECIES
                    out[row : row + SPECIES] = own[first + y, f, z]
            for z in range(CZ):
                row = SPECIES_ROWS + (y * CZ + z) * 8
                out[row : row + 8] = flow[first + y, z]
        for z in range(CZ):
            row = SPECIES_ROWS + FLOW_ROWS + z * 16
            out[row : row + 16] = noise_first[edge, z]


def flow_step(source, y, lane, keep):
    column = [source[y, z] for z in range(CZ)]
    above = [source[y + 1, z] for z in range(CZ)]
    below = [source[y - 1, z] for z in range(CZ)]
    row = lax.broadcasted_iota(jnp.int32, (8, NX), 0)
    results = []
    for z in range(CZ):
        total, change = stencil(column, above, below, z, lane)
        centre = column[z]
        moved = (
            source[y, z, 1:2] * change[0] + source[y, z, 2:3] * change[1] + source[y, z, 3:4] * change[2]
        )
        new = centre + time_step * viscosity * (total - 6.0 * centre) - speed_half * moved
        if keep is not None:
            new = new * keep
        results.append(jnp.where(row < 5, new, centre))
    return results


def transport(get, y, noise, noise_y, speeds, speeds_y, lane, emit):
    slow = [[speed_half * speeds[speeds_y, z, 1 + d : 2 + d] for d in range(3)] for z in range(CZ)]
    for f in range(FIELDS):
        column = [get(y, f, z) for z in range(CZ)]
        above = [get(y + 1, f, z) for z in range(CZ)]
        below = [get(y - 1, f, z) for z in range(CZ)]
        for z in range(CZ):
            total, change = stencil(column, above, below, z, lane)
            value = (1.0 - 6.0 * spread) * column[z] + spread * total
            for d in range(3):
                weight = noise_half * noise[noise_y, z, 3 * f + d : 3 * f + d + 1] - slow[z][d]
                value = value + weight * change[d]
            emit(f, z, value)


def store_halves(total, mine, other):
    core = lax.rem(lax.axis_index("field"), 2)
    for i in range(CZ // 2):
        mine[i] = total[core * 2 + i]
        other[i] = total[(1 - core) * 2 + i]


def join_halves(mine, other, total):
    core = lax.rem(lax.axis_index("field"), 2)
    for i in range(CZ // 2):
        total[core * 2 + i] = mine[i]
        total[(1 - core) * 2 + i] = other[i]


def first_step(
    own, flow, noise_first, low_halo, high_halo,
    carried, flow_one, mine, other,
    wide, wide_flow, wide_noise, total,
):
    tile = lax.axis_index("tile")
    last = lax.axis_size("tile") - 1
    lane, lane_flow = lanes((SPECIES, NX)), lanes((8, NX))
    wide[2 : CY + 2] = own[...]
    wide_flow[2 : CY + 2] = flow[...]
    wide_noise[1 : CY + 1] = noise_first[...]
    for halo, at, edge in ((low_halo, 0, 0), (high_halo, CY + 2, CY + 1)):
        wide[at : at + 2] = halo[0:SPECIES_ROWS].reshape(2, FIELDS, CZ, SPECIES, NX)
        wide_flow[at : at + 2] = halo[SPECIES_ROWS : SPECIES_ROWS + FLOW_ROWS].reshape(2, CZ, 8, NX)
        wide_noise[edge] = halo[SPECIES_ROWS + FLOW_ROWS :].reshape(CZ, 16, NX)

    def layer(y, _):
        outside = ((y == 0) & (tile == 0)) | ((y == CY + 1) & (tile == last))
        keep = jnp.where(outside, 0.0, 1.0).astype(f32)
        for z, new in enumerate(flow_step(wide_flow, y + 1, lane_flow, keep)):
            flow_one[y, z] = new
        sums = [None] * CZ

        def emit(f, z, value):
            value = value * keep
            carried[y, f, z] = value
            sums[z] = value if sums[z] is None else sums[z] + value

        transport(lambda at, f, z: wide[at, f, z], y + 1, wide_noise, y, flow_one, y, lane, emit)
        for z in range(CZ):
            total[z, y] = sums[z]
        return 0

    lax.fori_loop(0, CY + 2, layer, 0)
    store_halves(total, mine, other)


def prepare(reactants, stoich, weights):
    for j in range(SPECIES):
        product = reactants[j : j + 1] * stoich[...]
        high = product.astype(bf16)
        low = (product - high.astype(f32)).astype(bf16)
        weights[SPECIES * j : SPECIES * (j + 1)] = jnp.concatenate([high, low, high], 1)


def form(consts, flow, y, weights, rates, out, out_y):
    for z in range(CZ):
        level = flow[y, z, 4:5] - 1.0
        length = time_step / jnp.maximum(flow[y, z, 6:7], 1.0)
        rate = consts[0:REACT] * jnp.exp(consts[REACT : 2 * REACT] * level) * length
        high = rate.astype(bf16)
        low = (rate - high.astype(f32)).astype(bf16)
        at = slice(NX * z, NX * (z + 1))
        rates[0:REACT, at] = high
        rates[REACT : 2 * REACT, at] = high
        rates[2 * REACT : 3 * REACT, at] = low
    out[out_y] = jnp.dot(weights[...], rates[...], preferred_element_type=f32)


def react(matrices, y, z, flow, flow_y, values, held):
    count = jnp.broadcast_to(flow[flow_y, z, 6:7], (SPECIES, NX))
    for k in range(SUBS):
        for n, value in enumerate(values):
            held[z, n] = value
        changes = [None] * len(values)
        for j in range(SPECIES):
            block = matrices[y, SPECIES * j : SPECIES * (j + 1), NX * z : NX * (z + 1)]
            for n in range(len(values)):
                part = block * held[z, n, j : j + 1]
                changes[n] = part if changes[n] is None else changes[n] + part
        values = [value + jnp.where(count > float(k), change, 0.0) for value, change in zip(values, changes)]
    return values


def react_first(
    carried, flow_one, noise_second, wiener, reactants, stoich, consts,
    matrices, partial, mine, other,
    weights, rates, held, reacted, flow_two, total,
):
    prepare(reactants, stoich, weights)
    lane, lane_flow = lanes((SPECIES, NX)), lanes((8, NX))

    def react_layer(y, _):
        form(consts, flow_one, y, weights, rates, matrices, y)
        for z in range(CZ):
            values = react(matrices, y, z, flow_one, y, [carried[y, f, z] for f in range(FIELDS)], held)
            own_share = 1.0 - flow_one[y, z, 5:6]
            for f in range(FIELDS):
                reacted[y, f, z] = own_share * values[f]
        return 0

    lax.fori_loop(0, CY + 2, react_layer, 0)

    def layer(y, _):
        for z, new in enumerate(flow_step(flow_one, y + 1, lane_flow, None)):
            flow_two[y, z] = new
        sums = [None] * CZ

        def emit(f, z, value):
            partial[y, f, z] = value
            sums[z] = value if sums[z] is None else sums[z] + value

        transport(lambda at, f, z: reacted[at, f, z], y + 1, noise_second, y, flow_two, y, lane, emit)
        for z in range(CZ):
            total[z, pl.ds(y * SPECIES, SPECIES)] = sums[z]
        return 0

    lax.fori_loop(0, CY, layer, 0)
    for z in range(CZ):
        for d in range(3):
            rows = [384 + (f * 3 + d) * 32 + z * 8 for f in range(FIELDS)]
            total[z, 128 + 8 * d : 136 + 8 * d] = (
                (wiener[rows[0] : rows[0] + 8] + wiener[rows[1] : rows[1] + 8])
                + (wiener[rows[2] : rows[2] + 8] + wiener[rows[3] : rows[3] + 8])
            )
    store_halves(total, mine, other)


def add_sources(flow_tile, total, after, heat, molar):
    density = jnp.sum(molar * after, 0, keepdims=True) / ALL_FIELDS
    released = jnp.sum(heat * (after - total), 0, keepdims=True) / ALL_FIELDS
    row = lax.broadcasted_iota(jnp.int32, (8, NX), 0)
    with_density = flow_tile + time_step * relaxation * (density - flow_tile)
    return jnp.where(row == 0, with_density, jnp.where(row == 4, flow_tile + released, flow_tile))


def second_step(
    sum_mine, sum_other, flow_one, matrices, partial, noise_second, reactants, stoich, consts,
    matrices_two, own_part, shared, flow_two,
    total, flow_mid, weights, rates, held,
):
    prepare(reactants, stoich, weights)
    join_halves(sum_mine, sum_other, total)
    lane, lane_flow = lanes((SPECIES, NX)), lanes((8, NX))

    def mean_layer(y, _):
        for z in range(CZ):
            before = total[z, y]
            (after,) = react(matrices, y, z, flow_one, y, [before], held)
            shared[y, z] = (flow_one[y, z, 5:6] / ALL_FIELDS) * after
            flow_mid[y, z] = add_sources(
                flow_one[y, z], before, after, consts[192:208], consts[208:224]
            )
        return 0

    lax.fori_loop(0, CY + 2, mean_layer, 0)

    def layer(y, _):
        for z, new in enumerate(flow_step(flow_mid, y + 1, lane_flow, None)):
            flow_two[y, z] = new
        form(consts, flow_two, y, weights, rates, matrices_two, y)
        column = [shared[y + 1, z] for z in range(CZ)]
        above = [shared[y + 2, z] for z in range(CZ)]
        below = [shared[y, z] for z in range(CZ)]
        for z in range(CZ):
            neighbour_sum, change = stencil(column, above, below, z, lane)
            base = (1.0 - 6.0 * spread) * column[z] + spread * neighbour_sum
            slow = [speed_half * flow_two[y, z, 1 + d : 2 + d] for d in range(3)]
            values = []
            for f in range(FIELDS):
                value = partial[y, f, z] + base
                for d in range(3):
                    weight = noise_half * noise_second[y, z, 3 * f + d : 3 * f + d + 1] - slow[d]
                    value = value + weight * change[d]
                values.append(value)
            values = react(matrices_two, y, z, flow_two, y, values, held)
            own_share = 1.0 - flow_two[y, z, 5:6]
            for f in range(FIELDS):
                own_part[y, f, z] = own_share * values[f]
        return 0

    lax.fori_loop(0, CY, layer, 0)


def finish(
    sum_mine, sum_other, shared, flow_two, matrices_two, own_part, consts,
    flow_out, species_out,
    total, held,
):
    join_halves(sum_mine, sum_other, total)
    lane = lanes((SPECIES, NX))

    def layer(y, _):
        column = [shared[y + 1, z] for z in range(CZ)]
        above = [shared[y + 2, z] for z in range(CZ)]
        below = [shared[y, z] for z in range(CZ)]
        for z in range(CZ):
            neighbour_sum, change = stencil(column, above, below, z, lane)
            before = total[z, pl.ds(y * SPECIES, SPECIES)] + ALL_FIELDS * (
                (1.0 - 6.0 * spread) * column[z] + spread * neighbour_sum
            )
            for d in range(3):
                weight = (
                    noise_half * total[z, pl.ds(128 + 8 * d + y, 1)]
                    - ALL_FIELDS * speed_half * flow_two[y, z, 1 + d : 2 + d]
                )
                before = before + weight * change[d]
            (after,) = react(matrices_two, y, z, flow_two, y, [before], held)
            tile = add_sources(flow_two[y, z], before, after, consts[192:208], consts[208:224])
            for v in range(5):
                flow_out[v, z, pl.ds(y, 1)] = tile[v : v + 1]
            mean = (flow_two[y, z, 5:6] / ALL_FIELDS) * after
            for f in range(FIELDS):
                species_out[pl.ds(f * 512 + z * 8 + y, SPECIES, stride=32), :] = own_part[y, f, z] + mean
        return 0

    lax.fori_loop(0, CY, layer, 0)


def call(kernel, name, outs, scratch, flops, *operands):
    shapes = tuple(jax.ShapeDtypeStruct(shape, f32) for shape in outs)
    moved = sum(4 * math.prod(shape) for shape in outs) + sum(x.size * 4 for x in operands)
    return pl.pallas_call(
        kernel,
        out_shape=shapes,
        scratch_shapes=[pltpu.VMEM(*entry) for entry in scratch],
        cost_estimate=pl.CostEstimate(flops=flops, bytes_accessed=moved, transcendentals=0),
        compiler_params=pltpu.CompilerParams(vmem_limit_bytes=24 << 20),
        name=name,
    )(*operands)


def move(value, axis, pairs):
    return lax.ppermute(value, axis, pairs)


def field_total(mine, other):
    core_pairs = [(i, i ^ 1) for i in range(4)]
    chip_pairs = [(i, i ^ 2) for i in range(4)]
    mine = mine + move(other, "field", core_pairs)
    mine = mine + move(mine, "field", chip_pairs)
    return mine, move(mine, "field", core_pairs)


def on_device(
    density, velocity, energy, species, wiener, substeps, mix_rate,
    reactants, stoich, kinetic_constants, excitation_sensitivity, heat, molar,
):
    tiles = lax.axis_size("tile")
    wide = CY + 2
    noise_rows = wiener.reshape(-1, NX)
    consts = jnp.broadcast_to(
        jnp.concatenate([kinetic_constants, excitation_sensitivity, heat, molar])[:, None], (2 * REACT + 32, NX)
    )
    by_species = reactants.T
    grid = (FIELDS, CZ, SPECIES, NX)
    low, high, own, flow, noise_first, noise_second = call(
        pack, "pack",
        [(MESSAGE_ROWS, NX)] * 2 + [(CY,) + grid, (CY, CZ, 8, NX), (CY, CZ, 16, NX), (CY, CZ, 16, NX)],
        [], 10**6,
        species.reshape(-1, NX), density, velocity, energy, noise_rows, mix_rate, substeps,
    )
    low_halo = move(high, "tile", [(i, i + 1) for i in range(tiles - 1)])
    high_halo = move(low, "tile", [(i + 1, i) for i in range(tiles - 1)])
    carried, flow_one, mine, other = call(
        first_step, "first_step",
        [(wide,) + grid, (wide, CZ, 8, NX)] + [(2, wide, SPECIES, NX)] * 2,
        [((CY + 4,) + grid, f32), ((CY + 4, CZ, 8, NX), f32), ((wide, CZ, 16, NX), f32), ((CZ, wide, SPECIES, NX), f32)],
        10**7, own, flow, noise_first, low_halo, high_halo,
    )
    first_sum = field_total(mine, other)
    working = [((256, 3 * REACT), bf16), ((3 * REACT, CZ * NX), bf16)]
    held = ((CZ, FIELDS, SPECIES, NX), f32)
    matrices, partial, mine, other = call(
        react_first, "react_first",
        [(wide, 256, CZ * NX), (CY,) + grid] + [(2, 152, NX)] * 2,
        working + [held, ((wide,) + grid, f32), ((CY, CZ, 8, NX), f32), ((CZ, 152, NX), f32)],
        10**9, carried, flow_one, noise_second, noise_rows, by_species, stoich, consts,
    )
    second_sum = field_total(mine, other)
    matrices_two, own_part, shared, flow_two = call(
        second_step, "second_step",
        [(CY, 256, CZ * NX), (CY,) + grid, (wide, CZ, SPECIES, NX), (CY, CZ, 8, NX)],
        [((CZ, wide, SPECIES, NX), f32), ((wide, CZ, 8, NX), f32)] + working + [held],
        10**9, *first_sum, flow_one, matrices, partial, noise_second, by_species, stoich, consts,
    )
    flow_out, species_out = call(
        finish, "finish",
        [(5, CZ, CY, NX), (FIELDS * SPECIES * CZ * CY, NX)],
        [((CZ, 152, NX), f32), held],
        10**8, *second_sum, shared, flow_two, matrices_two, own_part, consts,
    )
    return flow_out[:, None], species_out.reshape(species.shape)


def solution(mesh):
    placed = (
        P("tile", None, None, None),
        P(None, "tile", None, None, None),
        P("tile", None, None, None),
        P("field", None, "tile", None, None, None),
        P(None, "field", None, "tile", None, None, None),
        P("tile", None, None, None),
        P("tile", None, None, None),
        P(),
        P(),
        P(),
        P(),
        P(),
        P(),
    )
    return jax.shard_map(
        on_device,
        mesh=mesh,
        in_specs=placed,
        out_specs=(P(None, "tile", None, None, None), P("field", None, "tile", None, None, None)),
        check_vma=False,
    )
```

```python
import math

import jax
import jax.numpy as jnp
from jax import lax
from jax.experimental import pallas as pl
from jax.experimental.pallas import tpu as pltpu
from jax.sharding import PartitionSpec as P

FIELDS = 4
SPECIES = 16
ALL_FIELDS = 16
REACT = 96
SUBS = 4
CZ, CY, NX = 4, 8, 128

time_step = 0.1
viscosity = 0.4
diffusivity = 0.3
relaxation = 2.0
noise_half = 0.5 * math.sqrt(2.0 * 0.3 * 0.1)
speed_half = 0.5 * time_step
spread = time_step * diffusivity
f32 = jnp.float32
bf16 = jnp.bfloat16

INNER, EDGES = CY - 2, 4
BUNDLE_ROWS = 2048 + 768 + 256
WEIGHTS = (256, 3 * REACT)
SPECIES_ROWS = 2 * FIELDS * CZ * SPECIES
FLOW_ROWS = 2 * CZ * 8
MESSAGE_ROWS = SPECIES_ROWS + FLOW_ROWS + CZ * 16


def lanes(shape):
    return lax.broadcasted_iota(jnp.int32, shape, 1)


def shift_x(value, lane):
    ahead = jnp.where(lane == NX - 1, 0.0, pltpu.roll(value, NX - 1, 1))
    behind = jnp.where(lane == 0, 0.0, pltpu.roll(value, 1, 1))
    return ahead, behind


def stencil(column, above, below, z, lane):
    zero = jnp.zeros_like(column[z])
    up = column[z + 1] if z + 1 < CZ else zero
    down = column[z - 1] if z > 0 else zero
    ahead, behind = shift_x(column[z], lane)
    total = (up + down) + (above[z] + below[z]) + (ahead + behind)
    return total, (up - down, above[z] - below[z], ahead - behind)


def start(copies, sems, first):
    started = [pltpu.make_async_copy(source, target, sems.at[first + n]) for n, (source, target) in enumerate(copies)]
    for one in started:
        one.start()
    return started


def flow_tiles(parts, flow):
    for z in range(CZ):
        rows = [part[z] for part in parts] + [jnp.zeros((CY, NX), f32)]
        rows[5] = time_step * rows[5]
        for v in range(8):
            flow[pl.ds(z * 8 + v, CY, stride=8 * CZ), :] = rows[v]


def noise_tile(wiener, first, step, y, z):
    rows = wiener[pl.ds(first + 384 * step + z * 8 + y, 12, stride=32), :]
    return jnp.concatenate([rows, jnp.zeros((4, NX), f32)], 0)


def pack(
    species_far, density_far, velocity_far, energy_far, wiener_far, mix_far, substeps_far,
    low, high, bundle,
    species, density, velocity, energy, wiener, mix, substeps, flow, sems,
):
    inputs = start([(species_far, species), (density_far, density), (velocity_far, velocity), (energy_far, energy),
                    (wiener_far, wiener), (mix_far, mix), (substeps_far, substeps)], sems, 0)
    for one in inputs:
        one.wait()
    passed = start([(species, bundle.at[0:2048]), (wiener, bundle.at[2048:2816])], sems, 7)
    parts = [density[0], velocity[0, 0], velocity[1, 0], velocity[2, 0], energy[0], mix[0], substeps[0].astype(f32)]
    flow_tiles(parts, flow)
    passed += start([(flow, bundle.at[2816:BUNDLE_ROWS])], sems, 9)
    for out, first, edge in ((low, 0, 0), (high, CY - 2, CY - 1)):
        for n in range(2):
            y = first + n
            for f in range(FIELDS):
                for z in range(CZ):
                    row = ((n * FIELDS + f) * CZ + z) * SPECIES
                    out[row : row + SPECIES] = species[pl.ds(f * 512 + z * 8 + y, SPECIES, stride=32), :]
            for z in range(CZ):
                row = SPECIES_ROWS + (n * CZ + z) * 8
                out[row : row + 8] = flow[(y * CZ + z) * 8 : (y * CZ + z + 1) * 8]
        for z in range(CZ):
            row = SPECIES_ROWS + FLOW_ROWS + z * 16
            out[row : row + 16] = noise_tile(wiener, 0, 0, edge, z)
    for one in passed:
        one.wait()


def flow_step(source, y, lane, keep):
    column = [source[y, z] for z in range(CZ)]
    above = [source[y + 1, z] for z in range(CZ)]
    below = [source[y - 1, z] for z in range(CZ)]
    row = lax.broadcasted_iota(jnp.int32, (8, NX), 0)
    results = []
    for z in range(CZ):
        total, change = stencil(column, above, below, z, lane)
        centre = column[z]
        moved = (
            source[y, z, 1:2] * change[0] + source[y, z, 2:3] * change[1] + source[y, z, 3:4] * change[2]
        )
        new = centre + time_step * viscosity * (total - 6.0 * centre) - speed_half * moved
        if keep is not None:
            new = new * keep
        results.append(jnp.where(row < 5, new, centre))
    return results


def transport(get, y, noise, noise_y, speeds, speeds_y, lane, emit):
    slow = [[speed_half * speeds[speeds_y, z, 1 + d : 2 + d] for d in range(3)] for z in range(CZ)]
    for f in range(FIELDS):
        column = [get(y, f, z) for z in range(CZ)]
        above = [get(y + 1, f, z) for z in range(CZ)]
        below = [get(y - 1, f, z) for z in range(CZ)]
        for z in range(CZ):
            total, change = stencil(column, above, below, z, lane)
            value = (1.0 - 6.0 * spread) * column[z] + spread * total
            for d in range(3):
                weight = noise_half * noise[noise_y, z, 3 * f + d : 3 * f + d + 1] - slow[z][d]
                value = value + weight * change[d]
            emit(f, z, value)


def store_halves(total, mine, other):
    core = lax.rem(lax.axis_index("field"), 2)
    for i in range(CZ // 2):
        mine[i] = total[core * 2 + i]
        other[i] = total[(1 - core) * 2 + i]


def join_halves(mine, other, total):
    core = lax.rem(lax.axis_index("field"), 2)
    for i in range(CZ // 2):
        total[core * 2 + i] = mine[i]
        total[(1 - core) * 2 + i] = other[i]


def first_edge(
    own, flow, noise_first, inner_flow, inner_sum, low_halo, high_halo,
    carried, flow_one, mine, other,
    wide, wide_flow, wide_noise, total,
):
    tile = lax.axis_index("tile")
    last = lax.axis_size("tile") - 1
    lane, lane_flow = lanes((SPECIES, NX)), lanes((8, NX))
    wide[2:4] = own[0:2]
    wide[4:6] = own[CY - 2 : CY]
    wide_flow[2:4] = flow[0:2]
    wide_flow[4:6] = flow[CY - 2 : CY]
    wide_noise[1] = noise_first[0]
    wide_noise[2] = noise_first[CY - 1]
    for halo, at, edge in ((low_halo, 0, 0), (high_halo, 6, 3)):
        wide[at : at + 2] = halo[0:SPECIES_ROWS].reshape(2, FIELDS, CZ, SPECIES, NX)
        wide_flow[at : at + 2] = halo[SPECIES_ROWS : SPECIES_ROWS + FLOW_ROWS].reshape(2, CZ, 8, NX)
        wide_noise[edge] = halo[SPECIES_ROWS + FLOW_ROWS :].reshape(CZ, 16, NX)
    flow_one[2:CY] = inner_flow[...]
    for z in range(CZ):
        total[z, 0:INNER] = inner_sum[z]

    def layer(e, _):
        outside = ((e == 0) & (tile == 0)) | ((e == 3) & (tile == last))
        keep = jnp.where(outside, 0.0, 1.0).astype(f32)
        high = e // 2
        centre, y = e + 1 + 2 * high, e + INNER * high
        for z, new in enumerate(flow_step(wide_flow, centre, lane_flow, keep)):
            flow_one[y, z] = new
        sums = [None] * CZ

        def emit(f, z, value):
            value = value * keep
            carried[e, f, z] = value
            sums[z] = value if sums[z] is None else sums[z] + value

        transport(lambda at, f, z: wide[at, f, z], centre, wide_noise, e, flow_one, y, lane, emit)
        for z in range(CZ):
            total[z, INNER + e] = sums[z]
        return 0

    lax.fori_loop(0, EDGES, layer, 0)
    store_halves(total, mine, other)


def prepare(consts, weights):
    stoich = consts[240:256, 0:REACT]
    for j in range(SPECIES):
        product = consts[224 + j : 225 + j, 0:REACT] * stoich
        high = product.astype(bf16)
        low = (product - high.astype(f32)).astype(bf16)
        weights[SPECIES * j : SPECIES * (j + 1)] = jnp.concatenate([high, low, high], 1)


def form(consts, flow, layers, weights, rates, out):
    for m, (y, _) in enumerate(layers):
        for z in range(CZ):
            level = flow[y, z, 4:5] - 1.0
            length = time_step / jnp.maximum(flow[y, z, 6:7], 1.0)
            rate = consts[0:REACT] * jnp.exp(consts[REACT : 2 * REACT] * level) * length
            high = rate.astype(bf16)
            low = (rate - high.astype(f32)).astype(bf16)
            at = slice(NX * (CZ * m + z), NX * (CZ * m + z + 1))
            rates[0:REACT, at] = high
            rates[REACT : 2 * REACT, at] = high
            rates[2 * REACT : 3 * REACT, at] = low
    product = jnp.dot(weights[...], rates[...], preferred_element_type=f32)
    for m, (_, n) in enumerate(layers):
        out[n] = product[:, CZ * NX * m : CZ * NX * (m + 1)]


def react(matrices, y, z, flow, flow_y, values, held):
    count = jnp.broadcast_to(flow[flow_y, z, 6:7], (SPECIES, NX))
    blocks = [matrices[y, SPECIES * j : SPECIES * (j + 1), NX * z : NX * (z + 1)] for j in range(SPECIES)]
    for k in range(SUBS):
        for n, value in enumerate(values):
            held[z, n] = value
        changes = [None] * len(values)
        for j in range(SPECIES):
            for n in range(len(values)):
                part = blocks[j] * held[z, n, j : j + 1]
                changes[n] = part if changes[n] is None else changes[n] + part
        values = [value + jnp.where(count > float(k), change, 0.0) for value, change in zip(values, changes)]
    return values


def react_own(flow, flow_y, matrices, y, carried, held, reacted):
    for z in range(CZ):
        values = react(matrices, y, z, flow, flow_y, [carried[y, f, z] for f in range(FIELDS)], held)
        own_share = 1.0 - flow[flow_y, z, 5:6]
        for f in range(FIELDS):
            reacted[y, f, z] = own_share * values[f]


def inner(
    bundle, consts,
    own, flow, noise_first, noise_second, noise_sum, flow_one, total, reacted, matrices, weights,
    carried, rates, held,
):
    lane, lane_flow = lanes((SPECIES, NX)), lanes((8, NX))
    prepare(consts, weights)
    flow[...] = bundle[2816:BUNDLE_ROWS].reshape(CY, CZ, 8, NX)

    def gather(y, _):
        for z in range(CZ):
            for f in range(FIELDS):
                own[y, f, z] = bundle[pl.ds(f * 512 + z * 8 + y, SPECIES, stride=32), :]
            noise_first[y, z] = noise_tile(bundle, 2048, 0, y, z)
            noise_second[y, z] = noise_tile(bundle, 2048, 1, y, z)
        return 0

    lax.fori_loop(0, CY, gather, 0)
    for z in range(CZ):
        for d in range(3):
            rows = [2048 + 384 + (f * 3 + d) * 32 + z * 8 for f in range(FIELDS)]
            noise_sum[z, 8 * d : 8 * d + 8] = (
                (bundle[rows[0] : rows[0] + 8] + bundle[rows[1] : rows[1] + 8])
                + (bundle[rows[2] : rows[2] + 8] + bundle[rows[3] : rows[3] + 8])
            )

    def layer(y, _):
        for z, new in enumerate(flow_step(flow, y + 1, lane_flow, None)):
            flow_one[y, z] = new
        sums = [None] * CZ

        def emit(f, z, value):
            carried[y, f, z] = value
            sums[z] = value if sums[z] is None else sums[z] + value

        transport(lambda at, f, z: own[at, f, z], y + 1, noise_first, y + 1, flow_one, y, lane, emit)
        for z in range(CZ):
            total[z, y] = sums[z]
        return 0

    lax.fori_loop(0, INNER, layer, 0)

    def form_group(g, _):
        form(consts, flow_one, [(3 * g + m, 3 * g + m) for m in range(3)], weights, rates, matrices)
        return 0

    lax.fori_loop(0, INNER // 3, form_group, 0)

    def react_layer(y, _):
        react_own(flow_one, y, matrices, y, carried, held, reacted)
        return 0

    lax.fori_loop(0, INNER, react_layer, 0)


def react_edge(
    carried, flow_one, inner_reacted, noise_second, noise_sum, weights, consts,
    matrices, partial, total,
    rates, held, edge_reacted, reacted, flow_two,
):
    lane, lane_flow = lanes((SPECIES, NX)), lanes((8, NX))

    def react_layer(e, _):
        react_own(flow_one, e + INNER * (e // 2), matrices, e, carried, held, edge_reacted)
        return 0

    form(consts, flow_one, [(0, 0), (1, 1), (CY, 2), (CY + 1, 3)], weights, rates, matrices)

    lax.fori_loop(0, EDGES, react_layer, 0)
    reacted[2:CY] = inner_reacted[...]
    reacted[0:2] = edge_reacted[0:2]
    reacted[CY : CY + 2] = edge_reacted[2:4]

    def layer(y, _):
        for z, new in enumerate(flow_step(flow_one, y + 1, lane_flow, None)):
            flow_two[y, z] = new
        sums = [None] * CZ

        def emit(f, z, value):
            partial[y, f, z] = value
            sums[z] = value if sums[z] is None else sums[z] + value

        transport(lambda at, f, z: reacted[at, f, z], y + 1, noise_second, y, flow_two, y, lane, emit)
        for z in range(CZ):
            total[z, pl.ds(y * SPECIES, SPECIES)] = sums[z]
        return 0

    lax.fori_loop(0, CY, layer, 0)
    for z in range(CZ):
        total[z, 128:152] = noise_sum[z]


def add_sources(flow_tile, total, after, heat, molar):
    density = jnp.sum(molar * after, 0, keepdims=True) / ALL_FIELDS
    released = jnp.sum(heat * (after - total), 0, keepdims=True) / ALL_FIELDS
    row = lax.broadcasted_iota(jnp.int32, (8, NX), 0)
    with_density = flow_tile + time_step * relaxation * (density - flow_tile)
    return jnp.where(row == 0, with_density, jnp.where(row == 4, flow_tile + released, flow_tile))


def second_step(
    sum_mine, sum_other, flow_one, inner_matrices, edge_matrices, partial, noise_second, weights, consts,
    matrices_two, own_part, shared, flow_two,
    total, flow_mid, rates, held,
):
    join_halves(sum_mine, sum_other, total)
    lane, lane_flow = lanes((SPECIES, NX)), lanes((8, NX))

    def mean_layer(matrices, n, at, y):
        for z in range(CZ):
            before = total[z, at]
            (after,) = react(matrices, n, z, flow_one, y, [before], held)
            shared[y, z] = (flow_one[y, z, 5:6] / ALL_FIELDS) * after
            flow_mid[y, z] = add_sources(
                flow_one[y, z], before, after, consts[192:208], consts[208:224]
            )

    def inner_layer(n, _):
        mean_layer(inner_matrices, n, n, n + 2)
        return 0

    def edge_layer(e, _):
        mean_layer(edge_matrices, e, INNER + e, e + INNER * (e // 2))
        return 0

    lax.fori_loop(0, INNER, inner_layer, 0)
    lax.fori_loop(0, EDGES, edge_layer, 0)

    def form_group(g, _):
        for m in range(4):
            for z, new in enumerate(flow_step(flow_mid, 4 * g + m + 1, lane_flow, None)):
                flow_two[4 * g + m, z] = new
        form(consts, flow_two, [(4 * g + m, 4 * g + m) for m in range(4)], weights, rates, matrices_two)
        return 0

    lax.fori_loop(0, CY // 4, form_group, 0)

    def layer(y, _):
        column = [shared[y + 1, z] for z in range(CZ)]
        above = [shared[y + 2, z] for z in range(CZ)]
        below = [shared[y, z] for z in range(CZ)]
        for z in range(CZ):
            neighbour_sum, change = stencil(column, above, below, z, lane)
            base = (1.0 - 6.0 * spread) * column[z] + spread * neighbour_sum
            slow = [speed_half * flow_two[y, z, 1 + d : 2 + d] for d in range(3)]
            values = []
            for f in range(FIELDS):
                value = partial[y, f, z] + base
                for d in range(3):
                    weight = noise_half * noise_second[y, z, 3 * f + d : 3 * f + d + 1] - slow[d]
                    value = value + weight * change[d]
                values.append(value)
            values = react(matrices_two, y, z, flow_two, y, values, held)
            own_share = 1.0 - flow_two[y, z, 5:6]
            for f in range(FIELDS):
                own_part[y, f, z] = own_share * values[f]
        return 0

    lax.fori_loop(0, CY, layer, 0)


def finish(
    sum_here, sum_there, shared, flow_two, matrices_two, own_part, consts,
    flow_out, species_out,
    total, held,
):
    total[...] = sum_here[...] + sum_there[...]
    lane = lanes((SPECIES, NX))

    def layer(y, _):
        column = [shared[y + 1, z] for z in range(CZ)]
        above = [shared[y + 2, z] for z in range(CZ)]
        below = [shared[y, z] for z in range(CZ)]
        for z in range(CZ):
            neighbour_sum, change = stencil(column, above, below, z, lane)
            before = total[z, pl.ds(y * SPECIES, SPECIES)] + ALL_FIELDS * (
                (1.0 - 6.0 * spread) * column[z] + spread * neighbour_sum
            )
            for d in range(3):
                weight = (
                    noise_half * total[z, pl.ds(128 + 8 * d + y, 1)]
                    - ALL_FIELDS * speed_half * flow_two[y, z, 1 + d : 2 + d]
                )
                before = before + weight * change[d]
            (after,) = react(matrices_two, y, z, flow_two, y, [before], held)
            tile = add_sources(flow_two[y, z], before, after, consts[192:208], consts[208:224])
            for v in range(5):
                flow_out[v, z, pl.ds(y, 1)] = tile[v : v + 1]
            mean = (flow_two[y, z, 5:6] / ALL_FIELDS) * after
            for f in range(FIELDS):
                species_out[pl.ds(f * 512 + z * 8 + y, SPECIES, stride=32), :] = own_part[y, f, z] + mean
        return 0

    lax.fori_loop(0, CY, layer, 0)


def call(kernel, name, outs, scratch, micros, *operands, far=0, far_outs=0, semaphores=0, weights_out=False, room=24):
    shapes = [jax.ShapeDtypeStruct(shape, f32) for shape in outs]
    if weights_out:
        shapes.append(jax.ShapeDtypeStruct(WEIGHTS, bf16))
    moved = sum(4 * math.prod(shape) for shape in outs) + sum(x.size * 4 for x in operands)
    places = [pl.BlockSpec(memory_space=pltpu.HBM if n < far else pltpu.VMEM) for n in range(len(operands))]
    out_places = [pl.BlockSpec(memory_space=pltpu.VMEM)] * (len(shapes) - far_outs)
    out_places += [pl.BlockSpec(memory_space=pltpu.HBM)] * far_outs
    semaphores = [pltpu.SemaphoreType.DMA((semaphores,))] if semaphores else []
    return pl.pallas_call(
        kernel,
        out_shape=tuple(shapes),
        in_specs=places,
        out_specs=tuple(out_places),
        scratch_shapes=[pltpu.VMEM(*entry) for entry in scratch] + semaphores,
        cost_estimate=pl.CostEstimate(flops=micros * 10**9, bytes_accessed=moved, transcendentals=0),
        compiler_params=pltpu.CompilerParams(vmem_limit_bytes=room << 20),
        name=name,
    )(*operands)


CORE_PAIRS = [(i, i ^ 1) for i in range(4)]
CHIP_PAIRS = [(i, i ^ 2) for i in range(4)]


def on_device(
    density, velocity, energy, species, wiener, substeps, mix_rate,
    reactants, stoich, kinetic_constants, excitation_sensitivity, heat, molar,
):
    tiles = lax.axis_size("tile")
    wide = CY + 2
    columns = jnp.concatenate([kinetic_constants, excitation_sensitivity, heat, molar])
    tables = jnp.concatenate([reactants.T, stoich], 0)
    consts = jnp.concatenate(
        [jnp.broadcast_to(columns[:, None], (2 * REACT + 32, NX)), jnp.pad(tables, ((0, 0), (0, NX - REACT)))], 0
    )
    grid = (FIELDS, CZ, SPECIES, NX)
    flow_grid, noise_grid = (CZ, 8, NX), (CZ, 16, NX)
    block = (1, CZ, CY, NX)
    fields = (species.reshape(-1, NX), density, velocity, energy, wiener.reshape(-1, NX), mix_rate, substeps)

    copies = [((2048, NX), f32), (block, f32), ((3,) + block, f32), (block, f32), ((768, NX), f32),
              (block, f32), (block, jnp.int32)]

    rates = ((3 * REACT, 4 * CZ * NX), bf16)
    held = ((CZ, FIELDS, SPECIES, NX), f32)
    low, high, bundle = call(
        pack, "pack", [(MESSAGE_ROWS, NX)] * 2 + [(BUNDLE_ROWS, NX)], copies + [((256, NX), f32)],
        2, *fields, far=7, far_outs=1, semaphores=10, room=64,
    )
    low_halo = lax.ppermute(high, "tile", [(i, i + 1) for i in range(tiles - 1)])
    high_halo = lax.ppermute(low, "tile", [(i + 1, i) for i in range(tiles - 1)])
    own, flow, noise_first, noise_second, noise_sum, inner_flow, inner_total, inner_reacted, inner_matrices, weights = call(
        inner, "inner",
        [(CY,) + grid, (CY,) + flow_grid, (CY,) + noise_grid, (CY,) + noise_grid, (CZ, 24, NX),
         (INNER,) + flow_grid, (CZ, INNER, SPECIES, NX), (INNER,) + grid, (INNER, 256, CZ * NX)],
        [((INNER,) + grid, f32), ((3 * REACT, 3 * CZ * NX), bf16), held],
        8, bundle, consts, weights_out=True,
    )
    carried, flow_one, mine, other = call(
        first_edge, "first_edge",
        [(EDGES,) + grid, (wide,) + flow_grid] + [(2, wide, SPECIES, NX)] * 2,
        [((8,) + grid, f32), ((8,) + flow_grid, f32), ((EDGES,) + noise_grid, f32), ((CZ, wide, SPECIES, NX), f32)],
        2, own, flow, noise_first, inner_flow, inner_total, low_halo, high_halo,
    )
    mine = mine + lax.ppermute(other, "field", CORE_PAIRS)
    mine, carried = lax.optimization_barrier((mine, carried))
    sum_mine = mine + lax.ppermute(mine, "field", CHIP_PAIRS)
    sum_other = lax.ppermute(sum_mine, "field", CORE_PAIRS)
    edge_matrices, partial, second = call(
        react_edge, "react_edge",
        [(EDGES, 256, CZ * NX), (CY,) + grid, (CZ, 152, NX)],
        [rates, held, ((EDGES,) + grid, f32), ((wide,) + grid, f32), ((CY,) + flow_grid, f32)],
        6, carried, flow_one, inner_reacted, noise_second, noise_sum, weights, consts,
    )
    second = second + lax.ppermute(second, "field", CORE_PAIRS)
    second_far = lax.ppermute(second, "field", CHIP_PAIRS)
    matrices_two, own_part, shared, flow_two = call(
        second_step, "second_step",
        [(CY, 256, CZ * NX), (CY,) + grid, (wide, CZ, SPECIES, NX), (CY,) + flow_grid],
        [((CZ, wide, SPECIES, NX), f32), ((wide,) + flow_grid, f32), rates, held],
        10, sum_mine, sum_other, flow_one, inner_matrices, edge_matrices, partial, noise_second, weights, consts,
    )
    flow_out, species_out = call(
        finish, "finish",
        [(5, CZ, CY, NX), (FIELDS * SPECIES * CZ * CY, NX)],
        [((CZ, 152, NX), f32), held],
        4, second, second_far, shared, flow_two, matrices_two, own_part, consts,
    )
    return flow_out[:, None], species_out.reshape(species.shape)


def solution(mesh):
    placed = (
        P("tile", None, None, None),
        P(None, "tile", None, None, None),
        P("tile", None, None, None),
        P("field", None, "tile", None, None, None),
        P(None, "field", None, "tile", None, None, None),
        P("tile", None, None, None),
        P("tile", None, None, None),
        P(),
        P(),
        P(),
        P(),
        P(),
        P(),
    )
    return jax.shard_map(
        on_device,
        mesh=mesh,
        in_specs=placed,
        out_specs=(P(None, "tile", None, None, None), P("field", None, "tile", None, None, None)),
        check_vma=False,
    )
```

```python
import math

import jax
import jax.numpy as jnp
from jax import lax
from jax.experimental import pallas as pl
from jax.experimental.pallas import tpu as pltpu
from jax.sharding import PartitionSpec as P

FIELDS = 4
SPECIES = 16
ALL_FIELDS = 16
REACT = 96
SUBS = 4
CZ, CY, NX = 4, 8, 128

time_step = 0.1
viscosity = 0.4
diffusivity = 0.3
relaxation = 2.0
noise_half = 0.5 * math.sqrt(2.0 * 0.3 * 0.1)
speed_half = 0.5 * time_step
spread = time_step * diffusivity
f32 = jnp.float32
bf16 = jnp.bfloat16

INNER, EDGES = CY - 2, 4
BUNDLE_ROWS = 2048 + 768 + 256 + 40
WEIGHTS = (256, 3 * REACT)
SPECIES_ROWS = 2 * FIELDS * CZ * SPECIES
FLOW_ROWS = 2 * CZ * 8
MESSAGE_ROWS = SPECIES_ROWS + FLOW_ROWS + CZ * 16


def lanes(shape):
    return lax.broadcasted_iota(jnp.int32, shape, 1)


def shift_x(value, lane):
    ahead = jnp.where(lane == NX - 1, 0.0, pltpu.roll(value, NX - 1, 1))
    behind = jnp.where(lane == 0, 0.0, pltpu.roll(value, 1, 1))
    return ahead, behind


def stencil(column, above, below, z, lane):
    zero = jnp.zeros_like(column[z])
    up = column[z + 1] if z + 1 < CZ else zero
    down = column[z - 1] if z > 0 else zero
    ahead, behind = shift_x(column[z], lane)
    total = (up + down) + (above[z] + below[z]) + (ahead + behind)
    return total, (up - down, above[z] - below[z], ahead - behind)


def start(copies, sems, first):
    started = [pltpu.make_async_copy(source, target, sems.at[first + n]) for n, (source, target) in enumerate(copies)]
    for one in started:
        one.start()
    return started


def flow_tiles(parts, flow):
    for z in range(CZ):
        rows = [part[z] for part in parts] + [jnp.zeros((CY, NX), f32)]
        rows[5] = time_step * rows[5]
        for v in range(8):
            flow[pl.ds(z * 8 + v, CY, stride=8 * CZ), :] = rows[v]


def noise_tile(wiener, first, step, y, z):
    rows = wiener[pl.ds(first + 384 * step + z * 8 + y, 12, stride=32), :]
    return jnp.concatenate([rows, jnp.zeros((4, NX), f32)], 0)


def pack(
    species_far, density_far, velocity_far, energy_far, wiener_far, mix_far, substeps_far,
    reactants_far, stoich_far, rate_far, excitation_far, heat_far, molar_far,
    low, high, bundle,
    species, density, velocity, energy, wiener, mix, substeps,
    reactants, stoich, rate, excitation, heat, molar, flow, table, sems,
):
    inputs = start([(species_far, species), (density_far, density), (velocity_far, velocity), (energy_far, energy),
                    (wiener_far, wiener), (mix_far, mix), (substeps_far, substeps),
                    (reactants_far, reactants), (stoich_far, stoich), (rate_far, rate), (excitation_far, excitation),
                    (heat_far, heat), (molar_far, molar)], sems, 0)
    for one in inputs:
        one.wait()
    passed = start([(species, bundle.at[0:2048]), (wiener, bundle.at[2048:2816])], sems, 13)
    table[...] = jnp.zeros_like(table)
    table[0:16, 0:REACT] = reactants[...]
    table[16:32, 0:REACT] = stoich[...]
    for n, vector in enumerate((rate, excitation)):
        table[32 + n : 33 + n, 0:REACT] = vector[...]
    for n, vector in enumerate((heat, molar)):
        table[34 + n : 35 + n, 0:SPECIES] = vector[...]
    parts = [density[0], velocity[0, 0], velocity[1, 0], velocity[2, 0], energy[0], mix[0], substeps[0].astype(f32)]
    flow_tiles(parts, flow)
    passed += start([(flow, bundle.at[2816:3072]), (table, bundle.at[3072:BUNDLE_ROWS])], sems, 15)
    for out, first, edge in ((low, 0, 0), (high, CY - 2, CY - 1)):
        for n in range(2):
            y = first + n
            for f in range(FIELDS):
                for z in range(CZ):
                    row = ((n * FIELDS + f) * CZ + z) * SPECIES
                    out[row : row + SPECIES] = species[pl.ds(f * 512 + z * 8 + y, SPECIES, stride=32), :]
            for z in range(CZ):
                row = SPECIES_ROWS + (n * CZ + z) * 8
                out[row : row + 8] = flow[(y * CZ + z) * 8 : (y * CZ + z + 1) * 8]
        for z in range(CZ):
            row = SPECIES_ROWS + FLOW_ROWS + z * 16
            out[row : row + 16] = noise_tile(wiener, 0, 0, edge, z)
    for one in passed:
        one.wait()


def flow_step(source, y, lane, keep):
    column = [source[y, z] for z in range(CZ)]
    above = [source[y + 1, z] for z in range(CZ)]
    below = [source[y - 1, z] for z in range(CZ)]
    row = lax.broadcasted_iota(jnp.int32, (8, NX), 0)
    results = []
    for z in range(CZ):
        total, change = stencil(column, above, below, z, lane)
        centre = column[z]
        moved = (
            source[y, z, 1:2] * change[0] + source[y, z, 2:3] * change[1] + source[y, z, 3:4] * change[2]
        )
        new = centre + time_step * viscosity * (total - 6.0 * centre) - speed_half * moved
        if keep is not None:
            new = new * keep
        results.append(jnp.where(row < 5, new, centre))
    return results


def transport(get, y, noise, noise_y, speeds, speeds_y, lane, emit):
    slow = [[speed_half * speeds[speeds_y, z, 1 + d : 2 + d] for d in range(3)] for z in range(CZ)]
    for f in range(FIELDS):
        column = [get(y, f, z) for z in range(CZ)]
        above = [get(y + 1, f, z) for z in range(CZ)]
        below = [get(y - 1, f, z) for z in range(CZ)]
        for z in range(CZ):
            total, change = stencil(column, above, below, z, lane)
            value = (1.0 - 6.0 * spread) * column[z] + spread * total
            for d in range(3):
                weight = noise_half * noise[noise_y, z, 3 * f + d : 3 * f + d + 1] - slow[z][d]
                value = value + weight * change[d]
            emit(f, z, value)


def store_halves(total, mine, other):
    core = lax.rem(lax.axis_index("field"), 2)
    for i in range(CZ // 2):
        mine[i] = total[core * 2 + i]
        other[i] = total[(1 - core) * 2 + i]


def join_halves(mine, other, total):
    core = lax.rem(lax.axis_index("field"), 2)
    for i in range(CZ // 2):
        total[core * 2 + i] = mine[i]
        total[(1 - core) * 2 + i] = other[i]


def first_edge(
    own, flow, noise_first, inner_flow, inner_sum, low_halo, high_halo,
    carried, flow_one, mine, other,
    wide, wide_flow, wide_noise, total,
):
    tile = lax.axis_index("tile")
    last = lax.axis_size("tile") - 1
    lane, lane_flow = lanes((SPECIES, NX)), lanes((8, NX))
    wide[2:4] = own[0:2]
    wide[4:6] = own[CY - 2 : CY]
    wide_flow[2:4] = flow[0:2]
    wide_flow[4:6] = flow[CY - 2 : CY]
    wide_noise[1] = noise_first[0]
    wide_noise[2] = noise_first[CY - 1]
    for halo, at, edge in ((low_halo, 0, 0), (high_halo, 6, 3)):
        wide[at : at + 2] = halo[0:SPECIES_ROWS].reshape(2, FIELDS, CZ, SPECIES, NX)
        wide_flow[at : at + 2] = halo[SPECIES_ROWS : SPECIES_ROWS + FLOW_ROWS].reshape(2, CZ, 8, NX)
        wide_noise[edge] = halo[SPECIES_ROWS + FLOW_ROWS :].reshape(CZ, 16, NX)
    flow_one[2:CY] = inner_flow[...]
    for z in range(CZ):
        total[z, 0:INNER] = inner_sum[z]

    def layer(e, _):
        outside = ((e == 0) & (tile == 0)) | ((e == 3) & (tile == last))
        keep = jnp.where(outside, 0.0, 1.0).astype(f32)
        high = e // 2
        centre, y = e + 1 + 2 * high, e + INNER * high
        for z, new in enumerate(flow_step(wide_flow, centre, lane_flow, keep)):
            flow_one[y, z] = new
        sums = [None] * CZ

        def emit(f, z, value):
            value = value * keep
            carried[e, f, z] = value
            sums[z] = value if sums[z] is None else sums[z] + value

        transport(lambda at, f, z: wide[at, f, z], centre, wide_noise, e, flow_one, y, lane, emit)
        for z in range(CZ):
            total[z, INNER + e] = sums[z]
        return 0

    lax.fori_loop(0, EDGES, layer, 0)
    store_halves(total, mine, other)


def prepare(bundle, consts, weights):
    for n, (at, size) in enumerate(((0, REACT), (REACT, REACT), (2 * REACT, SPECIES), (2 * REACT + 16, SPECIES))):
        square = jnp.broadcast_to(bundle[3104 + n : 3105 + n], (NX, NX)).T
        consts[at : at + size] = square[0:size]
    stoich = bundle[3088:3104, 0:REACT]
    for j in range(SPECIES):
        product = bundle[3072 + j : 3073 + j, 0:REACT] * stoich
        high = product.astype(bf16)
        low = (product - high.astype(f32)).astype(bf16)
        weights[SPECIES * j : SPECIES * (j + 1)] = jnp.concatenate([high, low, high], 1)


def form(consts, flow, layers, weights, rates, out):
    for m, (y, _) in enumerate(layers):
        for z in range(CZ):
            level = flow[y, z, 4:5] - 1.0
            length = time_step / jnp.maximum(flow[y, z, 6:7], 1.0)
            rate = consts[0:REACT] * jnp.exp(consts[REACT : 2 * REACT] * level) * length
            high = rate.astype(bf16)
            low = (rate - high.astype(f32)).astype(bf16)
            at = slice(NX * (CZ * m + z), NX * (CZ * m + z + 1))
            rates[0:REACT, at] = high
            rates[REACT : 2 * REACT, at] = high
            rates[2 * REACT : 3 * REACT, at] = low
    product = jnp.dot(weights[...], rates[...], preferred_element_type=f32)
    for m, (_, n) in enumerate(layers):
        out[n] = product[:, CZ * NX * m : CZ * NX * (m + 1)]


def react(matrices, y, z, flow, flow_y, values, held, place=None):
    place = z if place is None else place
    count = jnp.broadcast_to(flow[flow_y, z, 6:7], (SPECIES, NX))
    blocks = [matrices[y, SPECIES * j : SPECIES * (j + 1), NX * z : NX * (z + 1)] for j in range(SPECIES)]
    for k in range(SUBS):
        for n, value in enumerate(values):
            held[place, n] = value
        parts = 2 if len(values) == 1 else 1
        changes = [[None] * parts for _ in values]
        for j in range(SPECIES):
            for n, sums in enumerate(changes):
                part = blocks[j] * held[place, n, j : j + 1]
                sums[j % parts] = part if sums[j % parts] is None else sums[j % parts] + part
        changes = [sum(sums[1:], sums[0]) for sums in changes]
        values = [value + jnp.where(count > float(k), change, 0.0) for value, change in zip(values, changes)]
    return values


def react_own(flow, flow_y, matrices, y, carried, held, reacted):
    for z in range(CZ):
        values = react(matrices, y, z, flow, flow_y, [carried[y, f, z] for f in range(FIELDS)], held)
        own_share = 1.0 - flow[flow_y, z, 5:6]
        for f in range(FIELDS):
            reacted[y, f, z] = own_share * values[f]


def inner(
    bundle,
    own, flow, noise_first, noise_second, noise_sum, flow_one, total, reacted, matrices, consts, weights,
    carried, rates, held,
):
    lane, lane_flow = lanes((SPECIES, NX)), lanes((8, NX))
    prepare(bundle, consts, weights)
    flow[...] = bundle[2816:3072].reshape(CY, CZ, 8, NX)

    def gather(y, _):
        for z in range(CZ):
            for f in range(FIELDS):
                own[y, f, z] = bundle[pl.ds(f * 512 + z * 8 + y, SPECIES, stride=32), :]
            noise_first[y, z] = noise_tile(bundle, 2048, 0, y, z)
            noise_second[y, z] = noise_tile(bundle, 2048, 1, y, z)
        return 0

    lax.fori_loop(0, CY, gather, 0)
    for z in range(CZ):
        for d in range(3):
            rows = [2048 + 384 + (f * 3 + d) * 32 + z * 8 for f in range(FIELDS)]
            noise_sum[z, 8 * d : 8 * d + 8] = (
                (bundle[rows[0] : rows[0] + 8] + bundle[rows[1] : rows[1] + 8])
                + (bundle[rows[2] : rows[2] + 8] + bundle[rows[3] : rows[3] + 8])
            )

    def layer(y, _):
        for z, new in enumerate(flow_step(flow, y + 1, lane_flow, None)):
            flow_one[y, z] = new
        sums = [None] * CZ

        def emit(f, z, value):
            carried[y, f, z] = value
            sums[z] = value if sums[z] is None else sums[z] + value

        transport(lambda at, f, z: own[at, f, z], y + 1, noise_first, y + 1, flow_one, y, lane, emit)
        for z in range(CZ):
            total[z, y] = sums[z]
        return 0

    lax.fori_loop(0, INNER, layer, 0)

    def form_group(g, _):
        form(consts, flow_one, [(3 * g + m, 3 * g + m) for m in range(3)], weights, rates, matrices)
        return 0

    lax.fori_loop(0, INNER // 3, form_group, 0)

    def react_layer(y, _):
        react_own(flow_one, y, matrices, y, carried, held, reacted)
        return 0

    lax.fori_loop(0, INNER, react_layer, 0)


def react_edge(
    carried, flow_one, inner_reacted, noise_second, noise_sum, weights, consts,
    matrices, partial, total,
    rates, held, edge_reacted, reacted, flow_two,
):
    lane, lane_flow = lanes((SPECIES, NX)), lanes((8, NX))

    def react_layer(e, _):
        react_own(flow_one, e + INNER * (e // 2), matrices, e, carried, held, edge_reacted)
        return 0

    form(consts, flow_one, [(0, 0), (1, 1), (CY, 2), (CY + 1, 3)], weights, rates, matrices)

    lax.fori_loop(0, EDGES, react_layer, 0)
    reacted[2:CY] = inner_reacted[...]
    reacted[0:2] = edge_reacted[0:2]
    reacted[CY : CY + 2] = edge_reacted[2:4]

    def layer(y, _):
        for z, new in enumerate(flow_step(flow_one, y + 1, lane_flow, None)):
            flow_two[y, z] = new
        sums = [None] * CZ

        def emit(f, z, value):
            partial[y, f, z] = value
            sums[z] = value if sums[z] is None else sums[z] + value

        transport(lambda at, f, z: reacted[at, f, z], y + 1, noise_second, y, flow_two, y, lane, emit)
        for z in range(CZ):
            total[z, pl.ds(y * SPECIES, SPECIES)] = sums[z]
        return 0

    lax.fori_loop(0, CY, layer, 0)
    for z in range(CZ):
        total[z, 128:152] = noise_sum[z]


def add_sources(flow_tile, total, after, heat, molar):
    density = jnp.sum(molar * after, 0, keepdims=True) / ALL_FIELDS
    released = jnp.sum(heat * (after - total), 0, keepdims=True) / ALL_FIELDS
    row = lax.broadcasted_iota(jnp.int32, (8, NX), 0)
    with_density = flow_tile + time_step * relaxation * (density - flow_tile)
    return jnp.where(row == 0, with_density, jnp.where(row == 4, flow_tile + released, flow_tile))


def second_step(
    sum_mine, sum_other, flow_one, inner_matrices, edge_matrices, partial, noise_second, weights, consts,
    matrices_two, own_part, shared, flow_two,
    total, flow_mid, rates, held,
):
    join_halves(sum_mine, sum_other, total)
    lane, lane_flow = lanes((SPECIES, NX)), lanes((8, NX))

    def mean_layer(matrices, n, at, y):
        for z in range(CZ):
            before = total[z, at]
            (after,) = react(matrices, n, z, flow_one, y, [before], held)
            shared[y, z] = (flow_one[y, z, 5:6] / ALL_FIELDS) * after
            flow_mid[y, z] = add_sources(
                flow_one[y, z], before, after, consts[192:208], consts[208:224]
            )

    def inner_layer(n, _):
        mean_layer(inner_matrices, n, n, n + 2)
        return 0

    def edge_layer(e, _):
        mean_layer(edge_matrices, e, INNER + e, e + INNER * (e // 2))
        return 0

    lax.fori_loop(0, INNER, inner_layer, 0)
    lax.fori_loop(0, EDGES, edge_layer, 0)

    def form_group(g, _):
        for m in range(4):
            for z, new in enumerate(flow_step(flow_mid, 4 * g + m + 1, lane_flow, None)):
                flow_two[4 * g + m, z] = new
        form(consts, flow_two, [(4 * g + m, 4 * g + m) for m in range(4)], weights, rates, matrices_two)
        return 0

    lax.fori_loop(0, CY // 4, form_group, 0)

    def layer(y, _):
        column = [shared[y + 1, z] for z in range(CZ)]
        above = [shared[y + 2, z] for z in range(CZ)]
        below = [shared[y, z] for z in range(CZ)]
        for z in range(CZ):
            neighbour_sum, change = stencil(column, above, below, z, lane)
            base = (1.0 - 6.0 * spread) * column[z] + spread * neighbour_sum
            slow = [speed_half * flow_two[y, z, 1 + d : 2 + d] for d in range(3)]
            values = []
            for f in range(FIELDS):
                value = partial[y, f, z] + base
                for d in range(3):
                    weight = noise_half * noise_second[y, z, 3 * f + d : 3 * f + d + 1] - slow[d]
                    value = value + weight * change[d]
                values.append(value)
            values = react(matrices_two, y, z, flow_two, y, values, held)
            own_share = 1.0 - flow_two[y, z, 5:6]
            for f in range(FIELDS):
                own_part[y, f, z] = own_share * values[f]
        return 0

    lax.fori_loop(0, CY, layer, 0)


def finish(
    sum_here, sum_there, shared, flow_two, matrices_two, own_part, consts,
    flow_out, species_out,
    total, held, ready, sems,
):
    total[...] = sum_here[...] + sum_there[...]
    lane = lanes((SPECIES, NX))
    rows = ready.reshape(CZ * FIELDS * SPECIES * CY, NX)
    sent = []
    for z in range(CZ):

        def layers(g, _, z=z):
            for m in range(4):
                y = 4 * g + m
                column = {at: shared[y + 1, at] for at in range(max(z - 1, 0), min(z + 2, CZ))}
                neighbour_sum, change = stencil(column, {z: shared[y + 2, z]}, {z: shared[y, z]}, z, lane)
                before = total[z, pl.ds(y * SPECIES, SPECIES)] + ALL_FIELDS * (
                    (1.0 - 6.0 * spread) * column[z] + spread * neighbour_sum
                )
                for d in range(3):
                    weight = (
                        noise_half * total[z, pl.ds(128 + 8 * d + y, 1)]
                        - ALL_FIELDS * speed_half * flow_two[y, z, 1 + d : 2 + d]
                    )
                    before = before + weight * change[d]
                (after,) = react(matrices_two, y, z, flow_two, y, [before], held, m)
                tile = add_sources(flow_two[y, z], before, after, consts[192:208], consts[208:224])
                for v in range(5):
                    flow_out[v, z, pl.ds(y, 1)] = tile[v : v + 1]
                mean = (flow_two[y, z, 5:6] / ALL_FIELDS) * after
                for f in range(FIELDS):
                    rows[pl.ds((z * FIELDS + f) * SPECIES * CY + y, SPECIES, stride=CY), :] = own_part[y, f, z] + mean
            return 0

        lax.fori_loop(0, CY // 4, layers, 0)
        sent += start([(ready.at[z], species_out.at[:, z])], sems, z)
    for one in sent:
        one.wait()


def call(kernel, name, outs, scratch, micros, *operands, far=0, far_outs=0, semaphores=0, weights_out=False, room=24):
    shapes = [jax.ShapeDtypeStruct(shape, f32) for shape in outs]
    if weights_out:
        shapes.append(jax.ShapeDtypeStruct(WEIGHTS, bf16))
    moved = sum(4 * math.prod(shape) for shape in outs) + sum(x.size * 4 for x in operands)
    places = [pl.BlockSpec(memory_space=pltpu.HBM if n < far else pltpu.VMEM) for n in range(len(operands))]
    out_places = [pl.BlockSpec(memory_space=pltpu.VMEM)] * (len(shapes) - far_outs)
    out_places += [pl.BlockSpec(memory_space=pltpu.HBM)] * far_outs
    semaphores = [pltpu.SemaphoreType.DMA((semaphores,))] if semaphores else []
    return pl.pallas_call(
        kernel,
        out_shape=tuple(shapes),
        in_specs=places,
        out_specs=tuple(out_places),
        scratch_shapes=[pltpu.VMEM(*entry) for entry in scratch] + semaphores,
        cost_estimate=pl.CostEstimate(flops=micros * 10**9, bytes_accessed=moved, transcendentals=0),
        compiler_params=pltpu.CompilerParams(vmem_limit_bytes=room << 20),
        name=name,
    )(*operands)


CORE_PAIRS = [(i, i ^ 1) for i in range(4)]
CHIP_PAIRS = [(i, i ^ 2) for i in range(4)]


def on_device(
    density, velocity, energy, species, wiener, substeps, mix_rate,
    reactants, stoich, kinetic_constants, excitation_sensitivity, heat, molar,
):
    tiles = lax.axis_size("tile")
    wide = CY + 2
    vectors = (kinetic_constants, excitation_sensitivity, heat, molar)
    tables = (reactants.T, stoich) + tuple(vector[None] for vector in vectors)
    grid = (FIELDS, CZ, SPECIES, NX)
    flow_grid, noise_grid = (CZ, 8, NX), (CZ, 16, NX)
    block = (1, CZ, CY, NX)
    fields = (species.reshape(-1, NX), density, velocity, energy, wiener.reshape(-1, NX), mix_rate, substeps)

    copies = [((2048, NX), f32), (block, f32), ((3,) + block, f32), (block, f32), ((768, NX), f32),
              (block, f32), (block, jnp.int32)]
    copies += [(table.shape, f32) for table in tables]

    rates = ((3 * REACT, 4 * CZ * NX), bf16)
    held = ((CZ, FIELDS, SPECIES, NX), f32)
    low, high, bundle = call(
        pack, "pack", [(MESSAGE_ROWS, NX)] * 2 + [(BUNDLE_ROWS, NX)], copies + [((256, NX), f32), ((40, NX), f32)],
        2, *fields, *tables, far=13, far_outs=1, semaphores=17, room=64,
    )
    low_halo = lax.ppermute(high, "tile", [(i, i + 1) for i in range(tiles - 1)])
    high_halo = lax.ppermute(low, "tile", [(i + 1, i) for i in range(tiles - 1)])
    (
        own, flow, noise_first, noise_second, noise_sum, inner_flow, inner_total, inner_reacted, inner_matrices,
        consts, weights,
    ) = call(
        inner, "inner",
        [(CY,) + grid, (CY,) + flow_grid, (CY,) + noise_grid, (CY,) + noise_grid, (CZ, 24, NX),
         (INNER,) + flow_grid, (CZ, INNER, SPECIES, NX), (INNER,) + grid, (INNER, 256, CZ * NX), (224, NX)],
        [((INNER,) + grid, f32), ((3 * REACT, 3 * CZ * NX), bf16), held],
        8, bundle, weights_out=True,
    )
    carried, flow_one, mine, other = call(
        first_edge, "first_edge",
        [(EDGES,) + grid, (wide,) + flow_grid] + [(2, wide, SPECIES, NX)] * 2,
        [((8,) + grid, f32), ((8,) + flow_grid, f32), ((EDGES,) + noise_grid, f32), ((CZ, wide, SPECIES, NX), f32)],
        2, own, flow, noise_first, inner_flow, inner_total, low_halo, high_halo,
    )
    mine = mine + lax.ppermute(other, "field", CORE_PAIRS)
    mine, carried = lax.optimization_barrier((mine, carried))
    sum_mine = mine + lax.ppermute(mine, "field", CHIP_PAIRS)
    sum_other = lax.ppermute(sum_mine, "field", CORE_PAIRS)
    edge_matrices, partial, second = call(
        react_edge, "react_edge",
        [(EDGES, 256, CZ * NX), (CY,) + grid, (CZ, 152, NX)],
        [rates, held, ((EDGES,) + grid, f32), ((wide,) + grid, f32), ((CY,) + flow_grid, f32)],
        6, carried, flow_one, inner_reacted, noise_second, noise_sum, weights, consts,
    )
    second = second + lax.ppermute(second, "field", CORE_PAIRS)
    second_far = lax.ppermute(second, "field", CHIP_PAIRS)
    matrices_two, own_part, shared, flow_two = call(
        second_step, "second_step",
        [(CY, 256, CZ * NX), (CY,) + grid, (wide, CZ, SPECIES, NX), (CY,) + flow_grid],
        [((CZ, wide, SPECIES, NX), f32), ((wide,) + flow_grid, f32), rates, held],
        10, sum_mine, sum_other, flow_one, inner_matrices, edge_matrices, partial, noise_second, weights, consts,
    )
    flow_out, species_out = call(
        finish, "finish",
        [(5, CZ, CY, NX), (FIELDS * SPECIES, CZ, CY, NX)],
        [((CZ, 152, NX), f32), held, ((CZ, FIELDS * SPECIES, CY, NX), f32)],
        4, second, second_far, shared, flow_two, matrices_two, own_part, consts,
        far_outs=1, semaphores=CZ,
    )
    return flow_out[:, None], species_out.reshape(species.shape)


def solution(mesh):
    placed = (
        P("tile", None, None, None),
        P(None, "tile", None, None, None),
        P("tile", None, None, None),
        P("field", None, "tile", None, None, None),
        P(None, "field", None, "tile", None, None, None),
        P("tile", None, None, None),
        P("tile", None, None, None),
        P(),
        P(),
        P(),
        P(),
        P(),
        P(),
    )
    return jax.shard_map(
        on_device,
        mesh=mesh,
        in_specs=placed,
        out_specs=(P(None, "tile", None, None, None), P("field", None, "tile", None, None, None)),
        check_vma=False,
    )
```

```python
import math

import jax
import jax.numpy as jnp
from jax import lax
from jax.experimental import pallas as pl
from jax.experimental.pallas import tpu as pltpu
from jax.sharding import PartitionSpec as P

FIELDS = 4
SPECIES = 16
ALL_FIELDS = 16
REACT = 96
SUBS = 4
CZ, CY, NX = 4, 8, 128

time_step = 0.1
viscosity = 0.4
diffusivity = 0.3
relaxation = 2.0
noise_half = 0.5 * math.sqrt(2.0 * 0.3 * 0.1)
speed_half = 0.5 * time_step
spread = time_step * diffusivity
f32 = jnp.float32
bf16 = jnp.bfloat16

INNER, EDGES = CY - 2, 4
BUNDLE_ROWS = 2048 + 768 + 256 + 40
WEIGHTS = (256, 3 * REACT)
SPECIES_ROWS = 2 * FIELDS * CZ * SPECIES
FLOW_ROWS = 2 * CZ * 8
MESSAGE_ROWS = SPECIES_ROWS + FLOW_ROWS + CZ * 16


def lanes(shape):
    return lax.broadcasted_iota(jnp.int32, shape, 1)


def shift_x(value, lane):
    ahead = jnp.where(lane == NX - 1, 0.0, pltpu.roll(value, NX - 1, 1))
    behind = jnp.where(lane == 0, 0.0, pltpu.roll(value, 1, 1))
    return ahead, behind


def stencil(column, above, below, z, lane):
    zero = jnp.zeros_like(column[z])
    up = column[z + 1] if z + 1 < CZ else zero
    down = column[z - 1] if z > 0 else zero
    ahead, behind = shift_x(column[z], lane)
    total = (up + down) + (above[z] + below[z]) + (ahead + behind)
    return total, (up - down, above[z] - below[z], ahead - behind)


def start(copies, sems, first):
    started = [pltpu.make_async_copy(source, target, sems.at[first + n]) for n, (source, target) in enumerate(copies)]
    for one in started:
        one.start()
    return started


def flow_tiles(parts, flow):
    for z in range(CZ):
        rows = [part[z] for part in parts] + [jnp.zeros((CY, NX), f32)]
        rows[5] = time_step * rows[5]
        for v in range(8):
            flow[pl.ds(z * 8 + v, CY, stride=8 * CZ), :] = rows[v]


def noise_tile(wiener, first, step, y, z):
    rows = wiener[pl.ds(first + 384 * step + z * 8 + y, 12, stride=32), :]
    return jnp.concatenate([rows, jnp.zeros((4, NX), f32)], 0)


def pack(
    species_far, density_far, velocity_far, energy_far, wiener_far, mix_far, substeps_far,
    reactants_far, stoich_far, rate_far, excitation_far, heat_far, molar_far,
    low, high, bundle,
    species, density, velocity, energy, wiener, mix, substeps,
    reactants, stoich, rate, excitation, heat, molar, flow, table, low_held, high_held, sems,
):
    inputs = start([(species_far, species), (density_far, density), (velocity_far, velocity), (energy_far, energy),
                    (wiener_far, wiener), (mix_far, mix), (substeps_far, substeps),
                    (reactants_far, reactants), (stoich_far, stoich), (rate_far, rate), (excitation_far, excitation),
                    (heat_far, heat), (molar_far, molar)], sems, 0)
    for one in inputs:
        one.wait()
    passed = start([(species, bundle.at[0:2048]), (wiener, bundle.at[2048:2816])], sems, 13)
    table[...] = jnp.zeros_like(table)
    table[0:16, 0:REACT] = reactants[...]
    table[16:32, 0:REACT] = stoich[...]
    for n, vector in enumerate((rate, excitation)):
        table[32 + n : 33 + n, 0:REACT] = vector[...]
    for n, vector in enumerate((heat, molar)):
        table[34 + n : 35 + n, 0:SPECIES] = vector[...]
    parts = [density[0], velocity[0, 0], velocity[1, 0], velocity[2, 0], energy[0], mix[0], substeps[0].astype(f32)]
    flow_tiles(parts, flow)
    passed += start([(flow, bundle.at[2816:3072]), (table, bundle.at[3072:BUNDLE_ROWS])], sems, 15)
    for k, (out, sent, first, edge) in enumerate(((low_held, low, 0, 0), (high_held, high, CY - 2, CY - 1))):
        for n in range(2):
            y = first + n
            for f in range(FIELDS):
                for z in range(CZ):
                    row = ((n * FIELDS + f) * CZ + z) * SPECIES
                    out[row : row + SPECIES] = species[pl.ds(f * 512 + z * 8 + y, SPECIES, stride=32), :]
            for z in range(CZ):
                row = SPECIES_ROWS + (n * CZ + z) * 8
                out[row : row + 8] = flow[(y * CZ + z) * 8 : (y * CZ + z + 1) * 8]
        for z in range(CZ):
            row = SPECIES_ROWS + FLOW_ROWS + z * 16
            out[row : row + 16] = noise_tile(wiener, 0, 0, edge, z)
        passed += start([(out, sent)], sems, 17 + k)
    for one in passed:
        one.wait()


def flow_step(source, y, lane, keep):
    column = [source[y, z] for z in range(CZ)]
    above = [source[y + 1, z] for z in range(CZ)]
    below = [source[y - 1, z] for z in range(CZ)]
    row = lax.broadcasted_iota(jnp.int32, (8, NX), 0)
    results = []
    for z in range(CZ):
        total, change = stencil(column, above, below, z, lane)
        centre = column[z]
        moved = (
            source[y, z, 1:2] * change[0] + source[y, z, 2:3] * change[1] + source[y, z, 3:4] * change[2]
        )
        new = centre + time_step * viscosity * (total - 6.0 * centre) - speed_half * moved
        if keep is not None:
            new = new * keep
        results.append(jnp.where(row < 5, new, centre))
    return results


def transport(get, y, noise, noise_y, speeds, speeds_y, lane, emit):
    slow = [[speed_half * speeds[speeds_y, z, 1 + d : 2 + d] for d in range(3)] for z in range(CZ)]
    for f in range(FIELDS):
        column = [get(y, f, z) for z in range(CZ)]
        above = [get(y + 1, f, z) for z in range(CZ)]
        below = [get(y - 1, f, z) for z in range(CZ)]
        for z in range(CZ):
            total, change = stencil(column, above, below, z, lane)
            value = (1.0 - 6.0 * spread) * column[z] + spread * total
            for d in range(3):
                weight = noise_half * noise[noise_y, z, 3 * f + d : 3 * f + d + 1] - slow[z][d]
                value = value + weight * change[d]
            emit(f, z, value)


def store_halves(total, mine, other):
    core = lax.rem(lax.axis_index("field"), 2)
    for i in range(CZ // 2):
        mine[i] = total[core * 2 + i]
        other[i] = total[(1 - core) * 2 + i]


def join_halves(mine, other, total):
    core = lax.rem(lax.axis_index("field"), 2)
    for i in range(CZ // 2):
        total[core * 2 + i] = mine[i]
        total[(1 - core) * 2 + i] = other[i]


def first_edge(
    own, flow, noise_first, inner_flow, inner_sum, low_halo, high_halo,
    carried, flow_one, mine, other,
    wide, wide_flow, wide_noise, total,
):
    tile = lax.axis_index("tile")
    last = lax.axis_size("tile") - 1
    lane, lane_flow = lanes((SPECIES, NX)), lanes((8, NX))
    wide[2:4] = own[0:2]
    wide[4:6] = own[CY - 2 : CY]
    wide_flow[2:4] = flow[0:2]
    wide_flow[4:6] = flow[CY - 2 : CY]
    wide_noise[1] = noise_first[0]
    wide_noise[2] = noise_first[CY - 1]
    for halo, at, edge in ((low_halo, 0, 0), (high_halo, 6, 3)):
        wide[at : at + 2] = halo[0:SPECIES_ROWS].reshape(2, FIELDS, CZ, SPECIES, NX)
        wide_flow[at : at + 2] = halo[SPECIES_ROWS : SPECIES_ROWS + FLOW_ROWS].reshape(2, CZ, 8, NX)
        wide_noise[edge] = halo[SPECIES_ROWS + FLOW_ROWS :].reshape(CZ, 16, NX)
    flow_one[2:CY] = inner_flow[...]
    for z in range(CZ):
        total[z, 0:INNER] = inner_sum[z]

    def layer(e, _):
        outside = ((e == 0) & (tile == 0)) | ((e == 3) & (tile == last))
        keep = jnp.where(outside, 0.0, 1.0).astype(f32)
        high = e // 2
        centre, y = e + 1 + 2 * high, e + INNER * high
        for z, new in enumerate(flow_step(wide_flow, centre, lane_flow, keep)):
            flow_one[y, z] = new
        sums = [None] * CZ

        def emit(f, z, value):
            value = value * keep
            carried[e, f, z] = value
            sums[z] = value if sums[z] is None else sums[z] + value

        transport(lambda at, f, z: wide[at, f, z], centre, wide_noise, e, flow_one, y, lane, emit)
        for z in range(CZ):
            total[z, INNER + e] = sums[z]
        return 0

    lax.fori_loop(0, EDGES, layer, 0)
    store_halves(total, mine, other)


def prepare(bundle, consts, weights):
    for n, (at, size) in enumerate(((0, REACT), (REACT, REACT), (2 * REACT, SPECIES), (2 * REACT + 16, SPECIES))):
        square = jnp.broadcast_to(bundle[3104 + n : 3105 + n], (NX, NX)).T
        consts[at : at + size] = square[0:size]
    stoich = bundle[3088:3104, 0:REACT]
    for j in range(SPECIES):
        product = bundle[3072 + j : 3073 + j, 0:REACT] * stoich
        high = product.astype(bf16)
        low = (product - high.astype(f32)).astype(bf16)
        weights[SPECIES * j : SPECIES * (j + 1)] = jnp.concatenate([high, low, high], 1)


def form(consts, flow, layers, weights, rates, out):
    for m, (y, _) in enumerate(layers):
        for z in range(CZ):
            level = flow[y, z, 4:5] - 1.0
            length = time_step / jnp.maximum(flow[y, z, 6:7], 1.0)
            rate = consts[0:REACT] * jnp.exp(consts[REACT : 2 * REACT] * level) * length
            high = rate.astype(bf16)
            low = (rate - high.astype(f32)).astype(bf16)
            at = slice(NX * (CZ * m + z), NX * (CZ * m + z + 1))
            rates[0:REACT, at] = high
            rates[REACT : 2 * REACT, at] = high
            rates[2 * REACT : 3 * REACT, at] = low
    product = jnp.dot(weights[...], rates[...], preferred_element_type=f32)
    for m, (_, n) in enumerate(layers):
        out[n] = product[:, CZ * NX * m : CZ * NX * (m + 1)]


def react(matrices, y, z, flow, flow_y, values, held, place=None):
    place = z if place is None else place
    count = jnp.broadcast_to(flow[flow_y, z, 6:7], (SPECIES, NX))
    blocks = [matrices[y, SPECIES * j : SPECIES * (j + 1), NX * z : NX * (z + 1)] for j in range(SPECIES)]
    for k in range(SUBS):
        for n, value in enumerate(values):
            held[place, n] = value
        parts = 2 if len(values) == 1 else 1
        changes = [[None] * parts for _ in values]
        for j in range(SPECIES):
            for n, sums in enumerate(changes):
                part = blocks[j] * held[place, n, j : j + 1]
                sums[j % parts] = part if sums[j % parts] is None else sums[j % parts] + part
        changes = [sum(sums[1:], sums[0]) for sums in changes]
        values = [value + jnp.where(count > float(k), change, 0.0) for value, change in zip(values, changes)]
    return values


def react_own(flow, flow_y, matrices, y, carried, held, reacted):
    for z in range(CZ):
        values = react(matrices, y, z, flow, flow_y, [carried[y, f, z] for f in range(FIELDS)], held)
        own_share = 1.0 - flow[flow_y, z, 5:6]
        for f in range(FIELDS):
            reacted[y, f, z] = own_share * values[f]


def inner(
    bundle,
    own, flow, noise_first, noise_second, noise_sum, flow_one, total, reacted, matrices, consts, weights,
    carried, rates, held,
):
    lane, lane_flow = lanes((SPECIES, NX)), lanes((8, NX))
    prepare(bundle, consts, weights)
    flow[...] = bundle[2816:3072].reshape(CY, CZ, 8, NX)

    def gather(y, _):
        for z in range(CZ):
            for f in range(FIELDS):
                own[y, f, z] = bundle[pl.ds(f * 512 + z * 8 + y, SPECIES, stride=32), :]
            noise_first[y, z] = noise_tile(bundle, 2048, 0, y, z)
            noise_second[y, z] = noise_tile(bundle, 2048, 1, y, z)
        return 0

    lax.fori_loop(0, CY, gather, 0)
    for z in range(CZ):
        for d in range(3):
            rows = [2048 + 384 + (f * 3 + d) * 32 + z * 8 for f in range(FIELDS)]
            noise_sum[z, 8 * d : 8 * d + 8] = (
                (bundle[rows[0] : rows[0] + 8] + bundle[rows[1] : rows[1] + 8])
                + (bundle[rows[2] : rows[2] + 8] + bundle[rows[3] : rows[3] + 8])
            )

    def layer(y, _):
        for z, new in enumerate(flow_step(flow, y + 1, lane_flow, None)):
            flow_one[y, z] = new
        sums = [None] * CZ

        def emit(f, z, value):
            carried[y, f, z] = value
            sums[z] = value if sums[z] is None else sums[z] + value

        transport(lambda at, f, z: own[at, f, z], y + 1, noise_first, y + 1, flow_one, y, lane, emit)
        for z in range(CZ):
            total[z, y] = sums[z]
        return 0

    lax.fori_loop(0, INNER, layer, 0)

    def form_group(g, _):
        form(consts, flow_one, [(3 * g + m, 3 * g + m) for m in range(3)], weights, rates, matrices)
        return 0

    lax.fori_loop(0, INNER // 3, form_group, 0)

    def react_layer(y, _):
        react_own(flow_one, y, matrices, y, carried, held, reacted)
        return 0

    lax.fori_loop(0, INNER, react_layer, 0)


def react_edge(
    carried, flow_one, inner_reacted, noise_second, noise_sum, weights, consts,
    matrices, partial, total,
    rates, held, edge_reacted, reacted, flow_two,
):
    lane, lane_flow = lanes((SPECIES, NX)), lanes((8, NX))

    def react_layer(e, _):
        react_own(flow_one, e + INNER * (e // 2), matrices, e, carried, held, edge_reacted)
        return 0

    form(consts, flow_one, [(0, 0), (1, 1), (CY, 2), (CY + 1, 3)], weights, rates, matrices)

    lax.fori_loop(0, EDGES, react_layer, 0)
    reacted[2:CY] = inner_reacted[...]
    reacted[0:2] = edge_reacted[0:2]
    reacted[CY : CY + 2] = edge_reacted[2:4]

    def layer(y, _):
        for z, new in enumerate(flow_step(flow_one, y + 1, lane_flow, None)):
            flow_two[y, z] = new
        sums = [None] * CZ

        def emit(f, z, value):
            partial[y, f, z] = value
            sums[z] = value if sums[z] is None else sums[z] + value

        transport(lambda at, f, z: reacted[at, f, z], y + 1, noise_second, y, flow_two, y, lane, emit)
        for z in range(CZ):
            total[z, pl.ds(y * SPECIES, SPECIES)] = sums[z]
        return 0

    lax.fori_loop(0, CY, layer, 0)
    for z in range(CZ):
        total[z, 128:152] = noise_sum[z]


def add_sources(flow_tile, total, after, heat, molar):
    density = jnp.sum(molar * after, 0, keepdims=True) / ALL_FIELDS
    released = jnp.sum(heat * (after - total), 0, keepdims=True) / ALL_FIELDS
    row = lax.broadcasted_iota(jnp.int32, (8, NX), 0)
    with_density = flow_tile + time_step * relaxation * (density - flow_tile)
    return jnp.where(row == 0, with_density, jnp.where(row == 4, flow_tile + released, flow_tile))


def second_step(
    sum_mine, sum_other, flow_one, inner_matrices, edge_matrices, partial, noise_second, weights, consts,
    matrices_two, own_part, shared, flow_two,
    total, flow_mid, rates, held,
):
    join_halves(sum_mine, sum_other, total)
    lane, lane_flow = lanes((SPECIES, NX)), lanes((8, NX))

    def mean_layer(matrices, n, at, y, slot):
        for z in range(CZ):
            before = total[z, at]
            (after,) = react(matrices, n, z, flow_one, y, [before], held, slot * CZ + z)
            shared[y, z] = (flow_one[y, z, 5:6] / ALL_FIELDS) * after
            flow_mid[y, z] = add_sources(
                flow_one[y, z], before, after, consts[192:208], consts[208:224]
            )

    def inner_layer(n, _):
        for m in range(2):
            at = 2 * n + m
            mean_layer(inner_matrices, at, at, at + 2, m)
        return 0

    def edge_layer(e, _):
        for m in range(2):
            at = 2 * e + m
            mean_layer(edge_matrices, at, INNER + at, at + INNER * e, m)
        return 0

    lax.fori_loop(0, INNER // 2, inner_layer, 0)
    lax.fori_loop(0, EDGES // 2, edge_layer, 0)

    def form_group(g, _):
        for m in range(4):
            for z, new in enumerate(flow_step(flow_mid, 4 * g + m + 1, lane_flow, None)):
                flow_two[4 * g + m, z] = new
        form(consts, flow_two, [(4 * g + m, 4 * g + m) for m in range(4)], weights, rates, matrices_two)
        return 0

    lax.fori_loop(0, CY // 4, form_group, 0)

    def layer(y, _):
        column = [shared[y + 1, z] for z in range(CZ)]
        above = [shared[y + 2, z] for z in range(CZ)]
        below = [shared[y, z] for z in range(CZ)]
        for z in range(CZ):
            neighbour_sum, change = stencil(column, above, below, z, lane)
            base = (1.0 - 6.0 * spread) * column[z] + spread * neighbour_sum
            slow = [speed_half * flow_two[y, z, 1 + d : 2 + d] for d in range(3)]
            values = []
            for f in range(FIELDS):
                value = partial[y, f, z] + base
                for d in range(3):
                    weight = noise_half * noise_second[y, z, 3 * f + d : 3 * f + d + 1] - slow[d]
                    value = value + weight * change[d]
                values.append(value)
            values = react(matrices_two, y, z, flow_two, y, values, held)
            own_share = 1.0 - flow_two[y, z, 5:6]
            for f in range(FIELDS):
                own_part[y, f, z] = own_share * values[f]
        return 0

    lax.fori_loop(0, CY, layer, 0)


def finish(
    sum_here, sum_there, shared, flow_two, matrices_two, own_part, consts,
    flow_out, species_out,
    total, held, ready, sems,
):
    total[...] = sum_here[...] + sum_there[...]
    lane = lanes((SPECIES, NX))
    rows = ready.reshape(CZ * FIELDS * SPECIES * CY, NX)
    sent = []
    for z in range(CZ):

        def layers(g, _, z=z):
            for m in range(4):
                y = 4 * g + m
                column = {at: shared[y + 1, at] for at in range(max(z - 1, 0), min(z + 2, CZ))}
                neighbour_sum, change = stencil(column, {z: shared[y + 2, z]}, {z: shared[y, z]}, z, lane)
                before = total[z, pl.ds(y * SPECIES, SPECIES)] + ALL_FIELDS * (
                    (1.0 - 6.0 * spread) * column[z] + spread * neighbour_sum
                )
                for d in range(3):
                    weight = (
                        noise_half * total[z, pl.ds(128 + 8 * d + y, 1)]
                        - ALL_FIELDS * speed_half * flow_two[y, z, 1 + d : 2 + d]
                    )
                    before = before + weight * change[d]
                (after,) = react(matrices_two, y, z, flow_two, y, [before], held, m)
                tile = add_sources(flow_two[y, z], before, after, consts[192:208], consts[208:224])
                for v in range(5):
                    flow_out[v, z, pl.ds(y, 1)] = tile[v : v + 1]
                mean = (flow_two[y, z, 5:6] / ALL_FIELDS) * after
                for f in range(FIELDS):
                    rows[pl.ds((z * FIELDS + f) * SPECIES * CY + y, SPECIES, stride=CY), :] = own_part[y, f, z] + mean
            return 0

        lax.fori_loop(0, CY // 4, layers, 0)
        sent += start([(ready.at[z], species_out.at[:, z])], sems, z)
    for one in sent:
        one.wait()


def call(kernel, name, outs, scratch, micros, *operands, far=0, far_outs=0, semaphores=0, weights_out=False, room=24):
    shapes = [jax.ShapeDtypeStruct(shape, f32) for shape in outs]
    if weights_out:
        shapes.append(jax.ShapeDtypeStruct(WEIGHTS, bf16))
    moved = sum(4 * math.prod(shape) for shape in outs) + sum(x.size * 4 for x in operands)
    places = [pl.BlockSpec(memory_space=pltpu.HBM if n < far else pltpu.VMEM) for n in range(len(operands))]
    out_places = [pl.BlockSpec(memory_space=pltpu.VMEM)] * (len(shapes) - far_outs)
    out_places += [pl.BlockSpec(memory_space=pltpu.HBM)] * far_outs
    semaphores = [pltpu.SemaphoreType.DMA((semaphores,))] if semaphores else []
    return pl.pallas_call(
        kernel,
        out_shape=tuple(shapes),
        in_specs=places,
        out_specs=tuple(out_places),
        scratch_shapes=[pltpu.VMEM(*entry) for entry in scratch] + semaphores,
        cost_estimate=pl.CostEstimate(flops=micros * 10**9, bytes_accessed=moved, transcendentals=0),
        compiler_params=pltpu.CompilerParams(vmem_limit_bytes=room << 20),
        name=name,
    )(*operands)


CORE_PAIRS = [(i, i ^ 1) for i in range(4)]
CHIP_PAIRS = [(i, i ^ 2) for i in range(4)]


def on_device(
    density, velocity, energy, species, wiener, substeps, mix_rate,
    reactants, stoich, kinetic_constants, excitation_sensitivity, heat, molar,
):
    tiles = lax.axis_size("tile")
    wide = CY + 2
    vectors = (kinetic_constants, excitation_sensitivity, heat, molar)
    tables = (reactants.T, stoich) + tuple(vector[None] for vector in vectors)
    grid = (FIELDS, CZ, SPECIES, NX)
    flow_grid, noise_grid = (CZ, 8, NX), (CZ, 16, NX)
    block = (1, CZ, CY, NX)
    fields = (species.reshape(-1, NX), density, velocity, energy, wiener.reshape(-1, NX), mix_rate, substeps)

    copies = [((2048, NX), f32), (block, f32), ((3,) + block, f32), (block, f32), ((768, NX), f32),
              (block, f32), (block, jnp.int32)]
    copies += [(table.shape, f32) for table in tables]

    rates = ((3 * REACT, 4 * CZ * NX), bf16)
    held = ((2 * CZ, FIELDS, SPECIES, NX), f32)
    low, high, bundle = call(
        pack, "pack", [(MESSAGE_ROWS, NX)] * 2 + [(BUNDLE_ROWS, NX)], copies + [((256, NX), f32), ((40, NX), f32)] + [((MESSAGE_ROWS, NX), f32)] * 2,
        2, *fields, *tables, far=13, far_outs=3, semaphores=19, room=64,
    )
    low_halo = lax.ppermute(high, "tile", [(i, i + 1) for i in range(tiles - 1)])
    high_halo = lax.ppermute(low, "tile", [(i + 1, i) for i in range(tiles - 1)])
    (
        own, flow, noise_first, noise_second, noise_sum, inner_flow, inner_total, inner_reacted, inner_matrices,
        consts, weights,
    ) = call(
        inner, "inner",
        [(CY,) + grid, (CY,) + flow_grid, (CY,) + noise_grid, (CY,) + noise_grid, (CZ, 24, NX),
         (INNER,) + flow_grid, (CZ, INNER, SPECIES, NX), (INNER,) + grid, (INNER, 256, CZ * NX), (224, NX)],
        [((INNER,) + grid, f32), ((3 * REACT, 3 * CZ * NX), bf16), held],
        8, bundle, weights_out=True,
    )
    carried, flow_one, mine, other = call(
        first_edge, "first_edge",
        [(EDGES,) + grid, (wide,) + flow_grid] + [(2, wide, SPECIES, NX)] * 2,
        [((8,) + grid, f32), ((8,) + flow_grid, f32), ((EDGES,) + noise_grid, f32), ((CZ, wide, SPECIES, NX), f32)],
        2, own, flow, noise_first, inner_flow, inner_total, low_halo, high_halo,
    )
    mine = mine + lax.ppermute(other, "field", CORE_PAIRS)
    mine, carried = lax.optimization_barrier((mine, carried))
    sum_mine = mine + lax.ppermute(mine, "field", CHIP_PAIRS)
    sum_other = lax.ppermute(sum_mine, "field", CORE_PAIRS)
    edge_matrices, partial, second = call(
        react_edge, "react_edge",
        [(EDGES, 256, CZ * NX), (CY,) + grid, (CZ, 152, NX)],
        [rates, held, ((EDGES,) + grid, f32), ((wide,) + grid, f32), ((CY,) + flow_grid, f32)],
        6, carried, flow_one, inner_reacted, noise_second, noise_sum, weights, consts,
    )
    second = second + lax.ppermute(second, "field", CORE_PAIRS)
    second_far = lax.ppermute(second, "field", CHIP_PAIRS)
    matrices_two, own_part, shared, flow_two = call(
        second_step, "second_step",
        [(CY, 256, CZ * NX), (CY,) + grid, (wide, CZ, SPECIES, NX), (CY,) + flow_grid],
        [((CZ, wide, SPECIES, NX), f32), ((wide,) + flow_grid, f32), rates, held],
        10, sum_mine, sum_other, flow_one, inner_matrices, edge_matrices, partial, noise_second, weights, consts,
    )
    flow_out, species_out = call(
        finish, "finish",
        [(5, CZ, CY, NX), (FIELDS * SPECIES, CZ, CY, NX)],
        [((CZ, 152, NX), f32), held, ((CZ, FIELDS * SPECIES, CY, NX), f32)],
        4, second, second_far, shared, flow_two, matrices_two, own_part, consts,
        far_outs=1, semaphores=CZ,
    )
    return flow_out[:, None], species_out.reshape(species.shape)


def solution(mesh):
    placed = (
        P("tile", None, None, None),
        P(None, "tile", None, None, None),
        P("tile", None, None, None),
        P("field", None, "tile", None, None, None),
        P(None, "field", None, "tile", None, None, None),
        P("tile", None, None, None),
        P("tile", None, None, None),
        P(),
        P(),
        P(),
        P(),
        P(),
        P(),
    )
    return jax.shard_map(
        on_device,
        mesh=mesh,
        in_specs=placed,
        out_specs=(P(None, "tile", None, None, None), P("field", None, "tile", None, None, None)),
        check_vma=False,
    )
```

```python
import math

import jax
import jax.numpy as jnp
from jax import lax
from jax.experimental import pallas as pl
from jax.experimental.pallas import tpu as pltpu
from jax.sharding import PartitionSpec as P

FIELDS = 4
SPECIES = 16
ALL_FIELDS = 16
REACT = 96
SUBS = 4
CZ, CY, NX = 4, 8, 128

time_step = 0.1
viscosity = 0.4
diffusivity = 0.3
relaxation = 2.0
noise_half = 0.5 * math.sqrt(2.0 * 0.3 * 0.1)
speed_half = 0.5 * time_step
spread = time_step * diffusivity
f32 = jnp.float32
bf16 = jnp.bfloat16

INNER, EDGES = CY - 2, 4
BUNDLE_ROWS = 2048 + 768 + 256 + 40
WEIGHTS = (256, 3 * REACT)
SPECIES_ROWS = 2 * FIELDS * CZ * SPECIES
FLOW_ROWS = 2 * CZ * 8
MESSAGE_ROWS = SPECIES_ROWS + FLOW_ROWS + CZ * 16


def lanes(shape):
    return lax.broadcasted_iota(jnp.int32, shape, 1)


def shift_x(value, lane):
    ahead = jnp.where(lane == NX - 1, 0.0, pltpu.roll(value, NX - 1, 1))
    behind = jnp.where(lane == 0, 0.0, pltpu.roll(value, 1, 1))
    return ahead, behind


def stencil(column, above, below, z, lane):
    zero = jnp.zeros_like(column[z])
    up = column[z + 1] if z + 1 < CZ else zero
    down = column[z - 1] if z > 0 else zero
    ahead, behind = shift_x(column[z], lane)
    total = (up + down) + (above[z] + below[z]) + (ahead + behind)
    return total, (up - down, above[z] - below[z], ahead - behind)


def start(copies, sems, first):
    started = [pltpu.make_async_copy(source, target, sems.at[first + n]) for n, (source, target) in enumerate(copies)]
    for one in started:
        one.start()
    return started


def flow_tiles(parts, flow):
    for z in range(CZ):
        rows = [part[z] for part in parts] + [jnp.zeros((CY, NX), f32)]
        rows[5] = time_step * rows[5]
        for v in range(8):
            flow[pl.ds(z * 8 + v, CY, stride=8 * CZ), :] = rows[v]


def noise_tile(wiener, first, step, y, z):
    rows = wiener[pl.ds(first + 384 * step + z * 8 + y, 12, stride=32), :]
    return jnp.concatenate([rows, jnp.zeros((4, NX), f32)], 0)


def pack(
    species_far, density_far, velocity_far, energy_far, wiener_far, mix_far, substeps_far,
    reactants_far, stoich_far, rate_far, excitation_far, heat_far, molar_far,
    low, high, bundle,
    species, density, velocity, energy, wiener, mix, substeps,
    reactants, stoich, rate, excitation, heat, molar, flow, table, low_held, high_held, sems,
):
    inputs = start([(species_far, species), (density_far, density), (velocity_far, velocity), (energy_far, energy),
                    (wiener_far, wiener), (mix_far, mix), (substeps_far, substeps),
                    (reactants_far, reactants), (stoich_far, stoich), (rate_far, rate), (excitation_far, excitation),
                    (heat_far, heat), (molar_far, molar)], sems, 0)
    for one in inputs:
        one.wait()
    passed = start([(species, bundle.at[0:2048]), (wiener, bundle.at[2048:2816])], sems, 13)
    table[...] = jnp.zeros_like(table)
    table[0:16, 0:REACT] = reactants[...]
    table[16:32, 0:REACT] = stoich[...]
    for n, vector in enumerate((rate, excitation)):
        table[32 + n : 33 + n, 0:REACT] = vector[...]
    for n, vector in enumerate((heat, molar)):
        table[34 + n : 35 + n, 0:SPECIES] = vector[...]
    parts = [density[0], velocity[0, 0], velocity[1, 0], velocity[2, 0], energy[0], mix[0], substeps[0].astype(f32)]
    flow_tiles(parts, flow)
    passed += start([(flow, bundle.at[2816:3072]), (table, bundle.at[3072:BUNDLE_ROWS])], sems, 15)
    for k, (out, sent, first, edge) in enumerate(((low_held, low, 0, 0), (high_held, high, CY - 2, CY - 1))):
        for n in range(2):
            y = first + n
            for f in range(FIELDS):
                for z in range(CZ):
                    row = ((n * FIELDS + f) * CZ + z) * SPECIES
                    out[row : row + SPECIES] = species[pl.ds(f * 512 + z * 8 + y, SPECIES, stride=32), :]
            for z in range(CZ):
                row = SPECIES_ROWS + (n * CZ + z) * 8
                out[row : row + 8] = flow[(y * CZ + z) * 8 : (y * CZ + z + 1) * 8]
        for z in range(CZ):
            row = SPECIES_ROWS + FLOW_ROWS + z * 16
            out[row : row + 16] = noise_tile(wiener, 0, 0, edge, z)
        passed += start([(out, sent)], sems, 17 + k)
    for one in passed:
        one.wait()


def flow_step(source, y, lane, keep):
    column = [source[y, z] for z in range(CZ)]
    above = [source[y + 1, z] for z in range(CZ)]
    below = [source[y - 1, z] for z in range(CZ)]
    row = lax.broadcasted_iota(jnp.int32, (8, NX), 0)
    results = []
    for z in range(CZ):
        total, change = stencil(column, above, below, z, lane)
        centre = column[z]
        moved = (
            source[y, z, 1:2] * change[0] + source[y, z, 2:3] * change[1] + source[y, z, 3:4] * change[2]
        )
        new = centre + time_step * viscosity * (total - 6.0 * centre) - speed_half * moved
        if keep is not None:
            new = new * keep
        results.append(jnp.where(row < 5, new, centre))
    return results


def transport(get, y, noise, noise_y, speeds, speeds_y, lane, emit):
    slow = [[speed_half * speeds[speeds_y, z, 1 + d : 2 + d] for d in range(3)] for z in range(CZ)]
    for f in range(FIELDS):
        column = [get(y, f, z) for z in range(CZ)]
        above = [get(y + 1, f, z) for z in range(CZ)]
        below = [get(y - 1, f, z) for z in range(CZ)]
        for z in range(CZ):
            total, change = stencil(column, above, below, z, lane)
            value = (1.0 - 6.0 * spread) * column[z] + spread * total
            for d in range(3):
                weight = noise_half * noise[noise_y, z, 3 * f + d : 3 * f + d + 1] - slow[z][d]
                value = value + weight * change[d]
            emit(f, z, value)


def store_halves(total, mine, other):
    core = lax.rem(lax.axis_index("field"), 2)
    for i in range(CZ // 2):
        mine[i] = total[core * 2 + i]
        other[i] = total[(1 - core) * 2 + i]


def join_halves(mine, other, total):
    core = lax.rem(lax.axis_index("field"), 2)
    for i in range(CZ // 2):
        total[core * 2 + i] = mine[i]
        total[(1 - core) * 2 + i] = other[i]


def first_edge(
    own, flow, noise_first, inner_flow, inner_sum, low_halo, high_halo,
    carried, flow_one, mine, other,
    wide, wide_flow, wide_noise, total,
):
    tile = lax.axis_index("tile")
    last = lax.axis_size("tile") - 1
    lane, lane_flow = lanes((SPECIES, NX)), lanes((8, NX))
    wide[2:4] = own[0:2]
    wide[4:6] = own[CY - 2 : CY]
    wide_flow[2:4] = flow[0:2]
    wide_flow[4:6] = flow[CY - 2 : CY]
    wide_noise[1] = noise_first[0]
    wide_noise[2] = noise_first[CY - 1]
    for halo, at, edge in ((low_halo, 0, 0), (high_halo, 6, 3)):
        wide[at : at + 2] = halo[0:SPECIES_ROWS].reshape(2, FIELDS, CZ, SPECIES, NX)
        wide_flow[at : at + 2] = halo[SPECIES_ROWS : SPECIES_ROWS + FLOW_ROWS].reshape(2, CZ, 8, NX)
        wide_noise[edge] = halo[SPECIES_ROWS + FLOW_ROWS :].reshape(CZ, 16, NX)
    flow_one[2:CY] = inner_flow[...]
    for z in range(CZ):
        total[z, 0:INNER] = inner_sum[z]

    def layer(e, _):
        outside = ((e == 0) & (tile == 0)) | ((e == 3) & (tile == last))
        keep = jnp.where(outside, 0.0, 1.0).astype(f32)
        high = e // 2
        centre, y = e + 1 + 2 * high, e + INNER * high
        for z, new in enumerate(flow_step(wide_flow, centre, lane_flow, keep)):
            flow_one[y, z] = new
        sums = [None] * CZ

        def emit(f, z, value):
            value = value * keep
            carried[e, f, z] = value
            sums[z] = value if sums[z] is None else sums[z] + value

        transport(lambda at, f, z: wide[at, f, z], centre, wide_noise, e, flow_one, y, lane, emit)
        for z in range(CZ):
            total[z, INNER + e] = sums[z]
        return 0

    lax.fori_loop(0, EDGES, layer, 0)
    store_halves(total, mine, other)


def prepare(bundle, consts, weights):
    for n, (at, size) in enumerate(((0, REACT), (REACT, REACT), (2 * REACT, SPECIES), (2 * REACT + 16, SPECIES))):
        square = jnp.broadcast_to(bundle[3104 + n : 3105 + n], (NX, NX)).T
        consts[at : at + size] = square[0:size]
    stoich = bundle[3088:3104, 0:REACT]
    for j in range(SPECIES):
        product = bundle[3072 + j : 3073 + j, 0:REACT] * stoich
        high = product.astype(bf16)
        low = (product - high.astype(f32)).astype(bf16)
        weights[SPECIES * j : SPECIES * (j + 1)] = jnp.concatenate([high, low, high], 1)


def form(consts, flow, layers, weights, rates, out):
    for m, (y, _) in enumerate(layers):
        for z in range(CZ):
            level = flow[y, z, 4:5] - 1.0
            length = time_step / jnp.maximum(flow[y, z, 6:7], 1.0)
            rate = consts[0:REACT] * jnp.exp(consts[REACT : 2 * REACT] * level) * length
            high = rate.astype(bf16)
            low = (rate - high.astype(f32)).astype(bf16)
            at = slice(NX * (CZ * m + z), NX * (CZ * m + z + 1))
            rates[0:REACT, at] = high
            rates[REACT : 2 * REACT, at] = high
            rates[2 * REACT : 3 * REACT, at] = low
    product = jnp.dot(weights[...], rates[...], preferred_element_type=f32)
    for m, (_, n) in enumerate(layers):
        out[n] = product[:, CZ * NX * m : CZ * NX * (m + 1)]


def react(matrices, y, z, flow, flow_y, values, held, place=None):
    place = z if place is None else place
    count = jnp.broadcast_to(flow[flow_y, z, 6:7], (SPECIES, NX))
    blocks = [matrices[y, SPECIES * j : SPECIES * (j + 1), NX * z : NX * (z + 1)] for j in range(SPECIES)]
    for k in range(SUBS):
        for n, value in enumerate(values):
            held[place, n] = value
        parts = 2 if len(values) == 1 else 1
        changes = [[None] * parts for _ in values]
        for j in range(SPECIES):
            for n, sums in enumerate(changes):
                part = blocks[j] * held[place, n, j : j + 1]
                sums[j % parts] = part if sums[j % parts] is None else sums[j % parts] + part
        changes = [sum(sums[1:], sums[0]) for sums in changes]
        values = [value + jnp.where(count > float(k), change, 0.0) for value, change in zip(values, changes)]
    return values


def react_own(flow, flow_y, matrices, y, carried, held, reacted):
    for z in range(CZ):
        values = react(matrices, y, z, flow, flow_y, [carried[y, f, z] for f in range(FIELDS)], held)
        own_share = 1.0 - flow[flow_y, z, 5:6]
        for f in range(FIELDS):
            reacted[y, f, z] = own_share * values[f]


def inner(
    bundle,
    own, flow, noise_first, noise_second, noise_sum, flow_one, total, reacted, matrices, consts, weights,
    carried, rates, held,
):
    lane, lane_flow = lanes((SPECIES, NX)), lanes((8, NX))
    prepare(bundle, consts, weights)
    flow[...] = bundle[2816:3072].reshape(CY, CZ, 8, NX)

    def gather(y, _):
        for z in range(CZ):
            for f in range(FIELDS):
                own[y, f, z] = bundle[pl.ds(f * 512 + z * 8 + y, SPECIES, stride=32), :]
            noise_first[y, z] = noise_tile(bundle, 2048, 0, y, z)
            noise_second[y, z] = noise_tile(bundle, 2048, 1, y, z)
        return 0

    lax.fori_loop(0, CY, gather, 0)
    for z in range(CZ):
        for d in range(3):
            rows = [2048 + 384 + (f * 3 + d) * 32 + z * 8 for f in range(FIELDS)]
            noise_sum[z, 8 * d : 8 * d + 8] = (
                (bundle[rows[0] : rows[0] + 8] + bundle[rows[1] : rows[1] + 8])
                + (bundle[rows[2] : rows[2] + 8] + bundle[rows[3] : rows[3] + 8])
            )

    def layer(y, _):
        for z, new in enumerate(flow_step(flow, y + 1, lane_flow, None)):
            flow_one[y, z] = new
        sums = [None] * CZ

        def emit(f, z, value):
            carried[y, f, z] = value
            sums[z] = value if sums[z] is None else sums[z] + value

        transport(lambda at, f, z: own[at, f, z], y + 1, noise_first, y + 1, flow_one, y, lane, emit)
        for z in range(CZ):
            total[z, y] = sums[z]
        return 0

    lax.fori_loop(0, INNER, layer, 0)

    def form_group(g, _):
        form(consts, flow_one, [(3 * g + m, 3 * g + m) for m in range(3)], weights, rates, matrices)
        return 0

    lax.fori_loop(0, INNER // 3, form_group, 0)

    def react_layer(y, _):
        react_own(flow_one, y, matrices, y, carried, held, reacted)
        return 0

    lax.fori_loop(0, INNER, react_layer, 0)


def react_edge(
    carried, flow_one, inner_reacted, noise_second, noise_sum, weights, consts,
    matrices, partial, total,
    rates, held, edge_reacted, reacted, flow_two,
):
    lane, lane_flow = lanes((SPECIES, NX)), lanes((8, NX))

    def react_layer(e, _):
        react_own(flow_one, e + INNER * (e // 2), matrices, e, carried, held, edge_reacted)
        return 0

    form(consts, flow_one, [(0, 0), (1, 1), (CY, 2), (CY + 1, 3)], weights, rates, matrices)

    lax.fori_loop(0, EDGES, react_layer, 0)
    reacted[2:CY] = inner_reacted[...]
    reacted[0:2] = edge_reacted[0:2]
    reacted[CY : CY + 2] = edge_reacted[2:4]

    def layer(y, _):
        for z, new in enumerate(flow_step(flow_one, y + 1, lane_flow, None)):
            flow_two[y, z] = new
        sums = [None] * CZ

        def emit(f, z, value):
            partial[y, f, z] = value
            sums[z] = value if sums[z] is None else sums[z] + value

        transport(lambda at, f, z: reacted[at, f, z], y + 1, noise_second, y, flow_two, y, lane, emit)
        for z in range(CZ):
            total[z, pl.ds(y * SPECIES, SPECIES)] = sums[z]
        return 0

    lax.fori_loop(0, CY, layer, 0)
    for z in range(CZ):
        total[z, 128:152] = noise_sum[z]


def add_sources(flow_tile, total, after, heat, molar):
    density = jnp.sum(molar * after, 0, keepdims=True) / ALL_FIELDS
    released = jnp.sum(heat * (after - total), 0, keepdims=True) / ALL_FIELDS
    row = lax.broadcasted_iota(jnp.int32, (8, NX), 0)
    with_density = flow_tile + time_step * relaxation * (density - flow_tile)
    return jnp.where(row == 0, with_density, jnp.where(row == 4, flow_tile + released, flow_tile))


def second_step(
    sum_mine, sum_other, flow_one, inner_matrices, edge_matrices, partial, noise_second, weights, consts,
    matrices_two, own_part, shared, flow_two,
    total, flow_mid, rates, held,
):
    join_halves(sum_mine, sum_other, total)
    lane, lane_flow = lanes((SPECIES, NX)), lanes((8, NX))

    def mean_layer(matrices, n, at, y, slot):
        for z in range(CZ):
            before = total[z, at]
            (after,) = react(matrices, n, z, flow_one, y, [before], held, slot * CZ + z)
            shared[y, z] = (flow_one[y, z, 5:6] / ALL_FIELDS) * after
            flow_mid[y, z] = add_sources(
                flow_one[y, z], before, after, consts[192:208], consts[208:224]
            )

    def inner_layer(n, _):
        for m in range(2):
            at = 2 * n + m
            mean_layer(inner_matrices, at, at, at + 2, m)
        return 0

    def edge_layer(e, _):
        for m in range(2):
            at = 2 * e + m
            mean_layer(edge_matrices, at, INNER + at, at + INNER * e, m)
        return 0

    lax.fori_loop(0, INNER // 2, inner_layer, 0)
    lax.fori_loop(0, EDGES // 2, edge_layer, 0)

    def form_group(g, _):
        for m in range(4):
            for z, new in enumerate(flow_step(flow_mid, 4 * g + m + 1, lane_flow, None)):
                flow_two[4 * g + m, z] = new
        form(consts, flow_two, [(4 * g + m, 4 * g + m) for m in range(4)], weights, rates, matrices_two)
        return 0

    lax.fori_loop(0, CY // 4, form_group, 0)

    def layer(y, _):
        column = [shared[y + 1, z] for z in range(CZ)]
        above = [shared[y + 2, z] for z in range(CZ)]
        below = [shared[y, z] for z in range(CZ)]
        for z in range(CZ):
            neighbour_sum, change = stencil(column, above, below, z, lane)
            base = (1.0 - 6.0 * spread) * column[z] + spread * neighbour_sum
            slow = [speed_half * flow_two[y, z, 1 + d : 2 + d] for d in range(3)]
            values = []
            for f in range(FIELDS):
                value = partial[y, f, z] + base
                for d in range(3):
                    weight = noise_half * noise_second[y, z, 3 * f + d : 3 * f + d + 1] - slow[d]
                    value = value + weight * change[d]
                values.append(value)
            values = react(matrices_two, y, z, flow_two, y, values, held)
            own_share = 1.0 - flow_two[y, z, 5:6]
            for f in range(FIELDS):
                own_part[y, f, z] = own_share * values[f]
        return 0

    lax.fori_loop(0, CY, layer, 0)


def finish(
    sum_here, sum_there, shared, flow_two, matrices_two, own_part, consts,
    flow_out, species_out,
    total, held, ready, sems,
):
    total[...] = sum_here[...] + sum_there[...]
    lane = lanes((SPECIES, NX))
    rows = ready.reshape(CZ * FIELDS * SPECIES * CY, NX)
    sent = []
    for z in range(CZ):
        for y in range(CY):
            column = {at: shared[y + 1, at] for at in range(max(z - 1, 0), min(z + 2, CZ))}
            neighbour_sum, change = stencil(column, {z: shared[y + 2, z]}, {z: shared[y, z]}, z, lane)
            before = total[z, pl.ds(y * SPECIES, SPECIES)] + ALL_FIELDS * (
                (1.0 - 6.0 * spread) * column[z] + spread * neighbour_sum
            )
            for d in range(3):
                weight = (
                    noise_half * total[z, pl.ds(128 + 8 * d + y, 1)]
                    - ALL_FIELDS * speed_half * flow_two[y, z, 1 + d : 2 + d]
                )
                before = before + weight * change[d]
            (after,) = react(matrices_two, y, z, flow_two, y, [before], held, y)
            tile = add_sources(flow_two[y, z], before, after, consts[192:208], consts[208:224])
            for v in range(5):
                flow_out[v, z, pl.ds(y, 1)] = tile[v : v + 1]
            mean = (flow_two[y, z, 5:6] / ALL_FIELDS) * after
            for f in range(FIELDS):
                rows[pl.ds((z * FIELDS + f) * SPECIES * CY + y, SPECIES, stride=CY), :] = own_part[y, f, z] + mean
        sent += start([(ready.at[z], species_out.at[:, z])], sems, z)
    for one in sent:
        one.wait()


def call(kernel, name, outs, scratch, micros, *operands, far=0, far_outs=0, semaphores=0, weights_out=False, room=24):
    shapes = [jax.ShapeDtypeStruct(shape, f32) for shape in outs]
    if weights_out:
        shapes.append(jax.ShapeDtypeStruct(WEIGHTS, bf16))
    moved = sum(4 * math.prod(shape) for shape in outs) + sum(x.size * 4 for x in operands)
    places = [pl.BlockSpec(memory_space=pltpu.HBM if n < far else pltpu.VMEM) for n in range(len(operands))]
    out_places = [pl.BlockSpec(memory_space=pltpu.VMEM)] * (len(shapes) - far_outs)
    out_places += [pl.BlockSpec(memory_space=pltpu.HBM)] * far_outs
    semaphores = [pltpu.SemaphoreType.DMA((semaphores,))] if semaphores else []
    return pl.pallas_call(
        kernel,
        out_shape=tuple(shapes),
        in_specs=places,
        out_specs=tuple(out_places),
        scratch_shapes=[pltpu.VMEM(*entry) for entry in scratch] + semaphores,
        cost_estimate=pl.CostEstimate(flops=micros * 10**9, bytes_accessed=moved, transcendentals=0),
        compiler_params=pltpu.CompilerParams(vmem_limit_bytes=room << 20),
        name=name,
    )(*operands)


CORE_PAIRS = [(i, i ^ 1) for i in range(4)]
CHIP_PAIRS = [(i, i ^ 2) for i in range(4)]


def on_device(
    density, velocity, energy, species, wiener, substeps, mix_rate,
    reactants, stoich, kinetic_constants, excitation_sensitivity, heat, molar,
):
    tiles = lax.axis_size("tile")
    wide = CY + 2
    vectors = (kinetic_constants, excitation_sensitivity, heat, molar)
    tables = (reactants.T, stoich) + tuple(vector[None] for vector in vectors)
    grid = (FIELDS, CZ, SPECIES, NX)
    flow_grid, noise_grid = (CZ, 8, NX), (CZ, 16, NX)
    block = (1, CZ, CY, NX)
    fields = (species.reshape(-1, NX), density, velocity, energy, wiener.reshape(-1, NX), mix_rate, substeps)

    copies = [((2048, NX), f32), (block, f32), ((3,) + block, f32), (block, f32), ((768, NX), f32),
              (block, f32), (block, jnp.int32)]
    copies += [(table.shape, f32) for table in tables]

    rates = ((3 * REACT, 4 * CZ * NX), bf16)
    held = ((2 * CZ, FIELDS, SPECIES, NX), f32)
    low, high, bundle = call(
        pack, "pack", [(MESSAGE_ROWS, NX)] * 2 + [(BUNDLE_ROWS, NX)], copies + [((256, NX), f32), ((40, NX), f32)] + [((MESSAGE_ROWS, NX), f32)] * 2,
        2, *fields, *tables, far=13, far_outs=3, semaphores=19, room=64,
    )
    low_halo = lax.ppermute(high, "tile", [(i, i + 1) for i in range(tiles - 1)])
    high_halo = lax.ppermute(low, "tile", [(i + 1, i) for i in range(tiles - 1)])
    (
        own, flow, noise_first, noise_second, noise_sum, inner_flow, inner_total, inner_reacted, inner_matrices,
        consts, weights,
    ) = call(
        inner, "inner",
        [(CY,) + grid, (CY,) + flow_grid, (CY,) + noise_grid, (CY,) + noise_grid, (CZ, 24, NX),
         (INNER,) + flow_grid, (CZ, INNER, SPECIES, NX), (INNER,) + grid, (INNER, 256, CZ * NX), (224, NX)],
        [((INNER,) + grid, f32), ((3 * REACT, 3 * CZ * NX), bf16), held],
        8, bundle, weights_out=True,
    )
    carried, flow_one, mine, other = call(
        first_edge, "first_edge",
        [(EDGES,) + grid, (wide,) + flow_grid] + [(2, wide, SPECIES, NX)] * 2,
        [((8,) + grid, f32), ((8,) + flow_grid, f32), ((EDGES,) + noise_grid, f32), ((CZ, wide, SPECIES, NX), f32)],
        2, own, flow, noise_first, inner_flow, inner_total, low_halo, high_halo,
    )
    mine = mine + lax.ppermute(other, "field", CORE_PAIRS)
    mine, carried = lax.optimization_barrier((mine, carried))
    sum_mine = mine + lax.ppermute(mine, "field", CHIP_PAIRS)
    sum_other = lax.ppermute(sum_mine, "field", CORE_PAIRS)
    edge_matrices, partial, second = call(
        react_edge, "react_edge",
        [(EDGES, 256, CZ * NX), (CY,) + grid, (CZ, 152, NX)],
        [rates, held, ((EDGES,) + grid, f32), ((wide,) + grid, f32), ((CY,) + flow_grid, f32)],
        6, carried, flow_one, inner_reacted, noise_second, noise_sum, weights, consts,
    )
    second = second + lax.ppermute(second, "field", CORE_PAIRS)
    second_far = lax.ppermute(second, "field", CHIP_PAIRS)
    matrices_two, own_part, shared, flow_two = call(
        second_step, "second_step",
        [(CY, 256, CZ * NX), (CY,) + grid, (wide, CZ, SPECIES, NX), (CY,) + flow_grid],
        [((CZ, wide, SPECIES, NX), f32), ((wide,) + flow_grid, f32), rates, held],
        10, sum_mine, sum_other, flow_one, inner_matrices, edge_matrices, partial, noise_second, weights, consts,
    )
    flow_out, species_out = call(
        finish, "finish",
        [(5, CZ, CY, NX), (FIELDS * SPECIES, CZ, CY, NX)],
        [((CZ, 152, NX), f32), held, ((CZ, FIELDS * SPECIES, CY, NX), f32)],
        4, second, second_far, shared, flow_two, matrices_two, own_part, consts,
        far_outs=1, semaphores=CZ,
    )
    return flow_out[:, None], species_out.reshape(species.shape)


def solution(mesh):
    placed = (
        P("tile", None, None, None),
        P(None, "tile", None, None, None),
        P("tile", None, None, None),
        P("field", None, "tile", None, None, None),
        P(None, "field", None, "tile", None, None, None),
        P("tile", None, None, None),
        P("tile", None, None, None),
        P(),
        P(),
        P(),
        P(),
        P(),
        P(),
    )
    return jax.shard_map(
        on_device,
        mesh=mesh,
        in_specs=placed,
        out_specs=(P(None, "tile", None, None, None), P("field", None, "tile", None, None, None)),
        check_vma=False,
    )
```

```python
import math

import jax
import jax.numpy as jnp
from jax import lax
from jax.experimental import pallas as pl
from jax.experimental.pallas import tpu as pltpu
from jax.sharding import PartitionSpec as P

FIELDS = 4
SPECIES = 16
ALL_FIELDS = 16
REACT = 96
SUBS = 4
CZ, CY, NX = 4, 8, 128

time_step = 0.1
viscosity = 0.4
diffusivity = 0.3
relaxation = 2.0
noise_half = 0.5 * math.sqrt(2.0 * 0.3 * 0.1)
speed_half = 0.5 * time_step
spread = time_step * diffusivity
f32 = jnp.float32
bf16 = jnp.bfloat16

INNER, EDGES = CY - 2, 4
BUNDLE_ROWS = 2048 + 768 + 256 + 40
WEIGHTS = (256, 3 * REACT)
SPECIES_ROWS = 2 * FIELDS * CZ * SPECIES
FLOW_ROWS = 2 * CZ * 8
MESSAGE_ROWS = SPECIES_ROWS + FLOW_ROWS + CZ * 16


def lanes(shape):
    return lax.broadcasted_iota(jnp.int32, shape, 1)


def shift_x(value, lane):
    ahead = jnp.where(lane == NX - 1, 0.0, pltpu.roll(value, NX - 1, 1))
    behind = jnp.where(lane == 0, 0.0, pltpu.roll(value, 1, 1))
    return ahead, behind


def stencil(column, above, below, z, lane):
    zero = jnp.zeros_like(column[z])
    up = column[z + 1] if z + 1 < CZ else zero
    down = column[z - 1] if z > 0 else zero
    ahead, behind = shift_x(column[z], lane)
    total = (up + down) + (above[z] + below[z]) + (ahead + behind)
    return total, (up - down, above[z] - below[z], ahead - behind)


def start(copies, sems, first):
    started = [pltpu.make_async_copy(source, target, sems.at[first + n]) for n, (source, target) in enumerate(copies)]
    for one in started:
        one.start()
    return started


def flow_tiles(parts, flow):
    for z in range(CZ):
        rows = [part[z] for part in parts] + [jnp.zeros((CY, NX), f32)]
        rows[5] = time_step * rows[5]
        for v in range(8):
            flow[pl.ds(z * 8 + v, CY, stride=8 * CZ), :] = rows[v]


def noise_tile(wiener, first, step, y, z):
    rows = wiener[pl.ds(first + 384 * step + z * 8 + y, 12, stride=32), :]
    return jnp.concatenate([rows, jnp.zeros((4, NX), f32)], 0)


def pack(
    species_far, density_far, velocity_far, energy_far, wiener_far, mix_far, substeps_far,
    reactants_far, stoich_far, rate_far, excitation_far, heat_far, molar_far,
    low, high, bundle,
    species, density, velocity, energy, wiener, mix, substeps,
    reactants, stoich, rate, excitation, heat, molar, flow, table, low_held, high_held, sems,
):
    inputs = start([(species_far, species), (density_far, density), (velocity_far, velocity), (energy_far, energy),
                    (wiener_far, wiener), (mix_far, mix), (substeps_far, substeps),
                    (reactants_far, reactants), (stoich_far, stoich), (rate_far, rate), (excitation_far, excitation),
                    (heat_far, heat), (molar_far, molar)], sems, 0)
    for one in inputs:
        one.wait()
    passed = start([(species, bundle.at[0:2048]), (wiener, bundle.at[2048:2816])], sems, 13)
    table[...] = jnp.zeros_like(table)
    table[0:16, 0:REACT] = reactants[...]
    table[16:32, 0:REACT] = stoich[...]
    for n, vector in enumerate((rate, excitation)):
        table[32 + n : 33 + n, 0:REACT] = vector[...]
    for n, vector in enumerate((heat, molar)):
        table[34 + n : 35 + n, 0:SPECIES] = vector[...]
    parts = [density[0], velocity[0, 0], velocity[1, 0], velocity[2, 0], energy[0], mix[0], substeps[0].astype(f32)]
    flow_tiles(parts, flow)
    passed += start([(flow, bundle.at[2816:3072]), (table, bundle.at[3072:BUNDLE_ROWS])], sems, 15)
    for k, (out, sent, first, edge) in enumerate(((low_held, low, 0, 0), (high_held, high, CY - 2, CY - 1))):
        for n in range(2):
            y = first + n
            for f in range(FIELDS):
                for z in range(CZ):
                    row = ((n * FIELDS + f) * CZ + z) * SPECIES
                    out[row : row + SPECIES] = species[pl.ds(f * 512 + z * 8 + y, SPECIES, stride=32), :]
            for z in range(CZ):
                row = SPECIES_ROWS + (n * CZ + z) * 8
                out[row : row + 8] = flow[(y * CZ + z) * 8 : (y * CZ + z + 1) * 8]
        for z in range(CZ):
            row = SPECIES_ROWS + FLOW_ROWS + z * 16
            out[row : row + 16] = noise_tile(wiener, 0, 0, edge, z)
        passed += start([(out, sent)], sems, 17 + k)
    for one in passed:
        one.wait()


def flow_step(source, y, lane, keep):
    column = [source[y, z] for z in range(CZ)]
    above = [source[y + 1, z] for z in range(CZ)]
    below = [source[y - 1, z] for z in range(CZ)]
    row = lax.broadcasted_iota(jnp.int32, (8, NX), 0)
    results = []
    for z in range(CZ):
        total, change = stencil(column, above, below, z, lane)
        centre = column[z]
        moved = (
            source[y, z, 1:2] * change[0] + source[y, z, 2:3] * change[1] + source[y, z, 3:4] * change[2]
        )
        new = centre + time_step * viscosity * (total - 6.0 * centre) - speed_half * moved
        if keep is not None:
            new = new * keep
        results.append(jnp.where(row < 5, new, centre))
    return results


def transport(get, y, noise, noise_y, speeds, speeds_y, lane, emit):
    slow = [[speed_half * speeds[speeds_y, z, 1 + d : 2 + d] for d in range(3)] for z in range(CZ)]
    for f in range(FIELDS):
        column = [get(y, f, z) for z in range(CZ)]
        above = [get(y + 1, f, z) for z in range(CZ)]
        below = [get(y - 1, f, z) for z in range(CZ)]
        for z in range(CZ):
            total, change = stencil(column, above, below, z, lane)
            value = (1.0 - 6.0 * spread) * column[z] + spread * total
            for d in range(3):
                weight = noise_half * noise[noise_y, z, 3 * f + d : 3 * f + d + 1] - slow[z][d]
                value = value + weight * change[d]
            emit(f, z, value)


def store_halves(total, mine, other):
    core = lax.rem(lax.axis_index("field"), 2)
    for i in range(CZ // 2):
        mine[i] = total[core * 2 + i]
        other[i] = total[(1 - core) * 2 + i]


def join_halves(mine, other, total):
    core = lax.rem(lax.axis_index("field"), 2)
    for i in range(CZ // 2):
        total[core * 2 + i] = mine[i]
        total[(1 - core) * 2 + i] = other[i]


def first_edge(
    own, flow, noise_first, inner_flow, inner_sum, low_halo, high_halo,
    carried, flow_one, mine, other,
    wide, wide_flow, wide_noise, total,
):
    tile = lax.axis_index("tile")
    last = lax.axis_size("tile") - 1
    lane, lane_flow = lanes((SPECIES, NX)), lanes((8, NX))
    wide[2:4] = own[0:2]
    wide[4:6] = own[CY - 2 : CY]
    wide_flow[2:4] = flow[0:2]
    wide_flow[4:6] = flow[CY - 2 : CY]
    wide_noise[1] = noise_first[0]
    wide_noise[2] = noise_first[CY - 1]
    for halo, at, edge in ((low_halo, 0, 0), (high_halo, 6, 3)):
        wide[at : at + 2] = halo[0:SPECIES_ROWS].reshape(2, FIELDS, CZ, SPECIES, NX)
        wide_flow[at : at + 2] = halo[SPECIES_ROWS : SPECIES_ROWS + FLOW_ROWS].reshape(2, CZ, 8, NX)
        wide_noise[edge] = halo[SPECIES_ROWS + FLOW_ROWS :].reshape(CZ, 16, NX)
    flow_one[2:CY] = inner_flow[...]
    for z in range(CZ):
        total[z, 0:INNER] = inner_sum[z]

    def layer(e, _):
        outside = ((e == 0) & (tile == 0)) | ((e == 3) & (tile == last))
        keep = jnp.where(outside, 0.0, 1.0).astype(f32)
        high = e // 2
        centre, y = e + 1 + 2 * high, e + INNER * high
        for z, new in enumerate(flow_step(wide_flow, centre, lane_flow, keep)):
            flow_one[y, z] = new
        sums = [None] * CZ

        def emit(f, z, value):
            value = value * keep
            carried[e, f, z] = value
            sums[z] = value if sums[z] is None else sums[z] + value

        transport(lambda at, f, z: wide[at, f, z], centre, wide_noise, e, flow_one, y, lane, emit)
        for z in range(CZ):
            total[z, INNER + e] = sums[z]
        return 0

    lax.fori_loop(0, EDGES, layer, 0)
    store_halves(total, mine, other)


def prepare(bundle, consts, weights):
    for n, (at, size) in enumerate(((0, REACT), (REACT, REACT), (2 * REACT, SPECIES), (2 * REACT + 16, SPECIES))):
        square = jnp.broadcast_to(bundle[3104 + n : 3105 + n], (NX, NX)).T
        consts[at : at + size] = square[0:size]
    stoich = bundle[3088:3104, 0:REACT]
    for j in range(SPECIES):
        product = bundle[3072 + j : 3073 + j, 0:REACT] * stoich
        high = product.astype(bf16)
        low = (product - high.astype(f32)).astype(bf16)
        weights[SPECIES * j : SPECIES * (j + 1)] = jnp.concatenate([high, low, high], 1)


def form(consts, flow, layers, weights, rates, out):
    for m, (y, _) in enumerate(layers):
        for z in range(CZ):
            level = flow[y, z, 4:5] - 1.0
            length = time_step / jnp.maximum(flow[y, z, 6:7], 1.0)
            rate = consts[0:REACT] * jnp.exp(consts[REACT : 2 * REACT] * level) * length
            high = rate.astype(bf16)
            low = (rate - high.astype(f32)).astype(bf16)
            at = slice(NX * (CZ * m + z), NX * (CZ * m + z + 1))
            rates[0:REACT, at] = high
            rates[REACT : 2 * REACT, at] = high
            rates[2 * REACT : 3 * REACT, at] = low
    product = jnp.dot(weights[...], rates[...], preferred_element_type=f32)
    for m, (_, n) in enumerate(layers):
        out[n] = product[:, CZ * NX * m : CZ * NX * (m + 1)]


def react(matrices, y, z, flow, flow_y, values, held, place=None):
    place = z if place is None else place
    count = jnp.broadcast_to(flow[flow_y, z, 6:7], (SPECIES, NX))
    blocks = [matrices[y, SPECIES * j : SPECIES * (j + 1), NX * z : NX * (z + 1)] for j in range(SPECIES)]
    for k in range(SUBS):
        for n, value in enumerate(values):
            held[place, n] = value
        parts = 2 if len(values) == 1 else 1
        changes = [[None] * parts for _ in values]
        for j in range(SPECIES):
            for n, sums in enumerate(changes):
                part = blocks[j] * held[place, n, j : j + 1]
                sums[j % parts] = part if sums[j % parts] is None else sums[j % parts] + part
        changes = [sum(sums[1:], sums[0]) for sums in changes]
        values = [value + jnp.where(count > float(k), change, 0.0) for value, change in zip(values, changes)]
    return values


def react_own(flow, flow_y, matrices, y, carried, held, reacted):
    for z in range(CZ):
        values = react(matrices, y, z, flow, flow_y, [carried[y, f, z] for f in range(FIELDS)], held)
        own_share = 1.0 - flow[flow_y, z, 5:6]
        for f in range(FIELDS):
            reacted[y, f, z] = own_share * values[f]


def inner(
    bundle,
    own, flow, noise_first, noise_second, noise_sum, flow_one, total, reacted, matrices, consts, weights,
    carried, rates, held,
):
    lane, lane_flow = lanes((SPECIES, NX)), lanes((8, NX))
    prepare(bundle, consts, weights)
    flow[...] = bundle[2816:3072].reshape(CY, CZ, 8, NX)

    def gather(y, _):
        for z in range(CZ):
            for f in range(FIELDS):
                own[y, f, z] = bundle[pl.ds(f * 512 + z * 8 + y, SPECIES, stride=32), :]
            noise_first[y, z] = noise_tile(bundle, 2048, 0, y, z)
            noise_second[y, z] = noise_tile(bundle, 2048, 1, y, z)
        return 0

    lax.fori_loop(0, CY, gather, 0)
    for z in range(CZ):
        for d in range(3):
            rows = [2048 + 384 + (f * 3 + d) * 32 + z * 8 for f in range(FIELDS)]
            noise_sum[z, 8 * d : 8 * d + 8] = (
                (bundle[rows[0] : rows[0] + 8] + bundle[rows[1] : rows[1] + 8])
                + (bundle[rows[2] : rows[2] + 8] + bundle[rows[3] : rows[3] + 8])
            )

    def layer(y, _):
        for z, new in enumerate(flow_step(flow, y + 1, lane_flow, None)):
            flow_one[y, z] = new
        sums = [None] * CZ

        def emit(f, z, value):
            carried[y, f, z] = value
            sums[z] = value if sums[z] is None else sums[z] + value

        transport(lambda at, f, z: own[at, f, z], y + 1, noise_first, y + 1, flow_one, y, lane, emit)
        for z in range(CZ):
            total[z, y] = sums[z]
        return 0

    lax.fori_loop(0, INNER, layer, 0)

    def form_group(g, _):
        form(consts, flow_one, [(3 * g + m, 3 * g + m) for m in range(3)], weights, rates, matrices)
        return 0

    lax.fori_loop(0, INNER // 3, form_group, 0)

    def react_layer(y, _):
        react_own(flow_one, y, matrices, y, carried, held, reacted)
        return 0

    lax.fori_loop(0, INNER, react_layer, 0)


def react_edge(
    carried, flow_one, inner_reacted, noise_second, noise_sum, weights, consts,
    matrices, partial, total,
    rates, held, edge_reacted, reacted, flow_two,
):
    lane, lane_flow = lanes((SPECIES, NX)), lanes((8, NX))

    def react_layer(e, _):
        react_own(flow_one, e + INNER * (e // 2), matrices, e, carried, held, edge_reacted)
        return 0

    form(consts, flow_one, [(0, 0), (1, 1), (CY, 2), (CY + 1, 3)], weights, rates, matrices)

    lax.fori_loop(0, EDGES, react_layer, 0)
    reacted[2:CY] = inner_reacted[...]
    reacted[0:2] = edge_reacted[0:2]
    reacted[CY : CY + 2] = edge_reacted[2:4]

    def layer(y, _):
        for z, new in enumerate(flow_step(flow_one, y + 1, lane_flow, None)):
            flow_two[y, z] = new
        sums = [None] * CZ

        def emit(f, z, value):
            partial[y, f, z] = value
            sums[z] = value if sums[z] is None else sums[z] + value

        transport(lambda at, f, z: reacted[at, f, z], y + 1, noise_second, y, flow_two, y, lane, emit)
        for z in range(CZ):
            total[z, pl.ds(y * SPECIES, SPECIES)] = sums[z]
        return 0

    lax.fori_loop(0, CY, layer, 0)
    for z in range(CZ):
        total[z, 128:152] = noise_sum[z]


def add_sources(flow_tile, total, after, heat, molar):
    density = jnp.sum(molar * after, 0, keepdims=True) / ALL_FIELDS
    released = jnp.sum(heat * (after - total), 0, keepdims=True) / ALL_FIELDS
    row = lax.broadcasted_iota(jnp.int32, (8, NX), 0)
    with_density = flow_tile + time_step * relaxation * (density - flow_tile)
    return jnp.where(row == 0, with_density, jnp.where(row == 4, flow_tile + released, flow_tile))


def second_step(
    sum_mine, sum_other, flow_one, inner_matrices, edge_matrices, partial, noise_second, weights, consts,
    matrices_two, own_part, shared, flow_two,
    total, flow_mid, rates, held,
):
    join_halves(sum_mine, sum_other, total)
    lane, lane_flow = lanes((SPECIES, NX)), lanes((8, NX))

    def mean_layer(matrices, n, at, y, slot):
        for z in range(CZ):
            before = total[z, at]
            (after,) = react(matrices, n, z, flow_one, y, [before], held, slot * CZ + z)
            shared[y, z] = (flow_one[y, z, 5:6] / ALL_FIELDS) * after
            flow_mid[y, z] = add_sources(
                flow_one[y, z], before, after, consts[192:208], consts[208:224]
            )

    def inner_layer(n, _):
        for m in range(3):
            at = 3 * n + m
            mean_layer(inner_matrices, at, at, at + 2, m)
        return 0

    def edge_layer(e, _):
        for m in range(2):
            at = 2 * e + m
            mean_layer(edge_matrices, at, INNER + at, at + INNER * e, m)
        return 0

    lax.fori_loop(0, INNER // 3, inner_layer, 0)
    lax.fori_loop(0, EDGES // 2, edge_layer, 0)

    def form_group(g, _):
        for m in range(4):
            for z, new in enumerate(flow_step(flow_mid, 4 * g + m + 1, lane_flow, None)):
                flow_two[4 * g + m, z] = new
        form(consts, flow_two, [(4 * g + m, 4 * g + m) for m in range(4)], weights, rates, matrices_two)
        return 0

    lax.fori_loop(0, CY // 4, form_group, 0)

    def layer(y, _):
        column = [shared[y + 1, z] for z in range(CZ)]
        above = [shared[y + 2, z] for z in range(CZ)]
        below = [shared[y, z] for z in range(CZ)]
        for z in range(CZ):
            neighbour_sum, change = stencil(column, above, below, z, lane)
            base = (1.0 - 6.0 * spread) * column[z] + spread * neighbour_sum
            slow = [speed_half * flow_two[y, z, 1 + d : 2 + d] for d in range(3)]
            values = []
            for f in range(FIELDS):
                value = partial[y, f, z] + base
                for d in range(3):
                    weight = noise_half * noise_second[y, z, 3 * f + d : 3 * f + d + 1] - slow[d]
                    value = value + weight * change[d]
                values.append(value)
            values = react(matrices_two, y, z, flow_two, y, values, held)
            own_share = 1.0 - flow_two[y, z, 5:6]
            for f in range(FIELDS):
                own_part[y, f, z] = own_share * values[f]
        return 0

    lax.fori_loop(0, CY, layer, 0)


def finish(
    sum_here, sum_there, shared, flow_two, matrices_two, own_part, consts,
    flow_out, species_out,
    total, held, ready, sems,
):
    total[...] = sum_here[...] + sum_there[...]
    lane = lanes((SPECIES, NX))
    rows = ready.reshape(CZ * FIELDS * SPECIES * CY, NX)
    sent = []
    for z in range(CZ):
        for y in range(CY):
            column = {at: shared[y + 1, at] for at in range(max(z - 1, 0), min(z + 2, CZ))}
            neighbour_sum, change = stencil(column, {z: shared[y + 2, z]}, {z: shared[y, z]}, z, lane)
            before = total[z, pl.ds(y * SPECIES, SPECIES)] + ALL_FIELDS * (
                (1.0 - 6.0 * spread) * column[z] + spread * neighbour_sum
            )
            for d in range(3):
                weight = (
                    noise_half * total[z, pl.ds(128 + 8 * d + y, 1)]
                    - ALL_FIELDS * speed_half * flow_two[y, z, 1 + d : 2 + d]
                )
                before = before + weight * change[d]
            (after,) = react(matrices_two, y, z, flow_two, y, [before], held, y)
            tile = add_sources(flow_two[y, z], before, after, consts[192:208], consts[208:224])
            for v in range(5):
                flow_out[v, z, pl.ds(y, 1)] = tile[v : v + 1]
            mean = (flow_two[y, z, 5:6] / ALL_FIELDS) * after
            for f in range(FIELDS):
                rows[pl.ds((z * FIELDS + f) * SPECIES * CY + y, SPECIES, stride=CY), :] = own_part[y, f, z] + mean
        sent += start([(ready.at[z], species_out.at[:, z])], sems, z)
    for one in sent:
        one.wait()


def call(kernel, name, outs, scratch, micros, *operands, far=0, far_outs=0, semaphores=0, weights_out=False, room=24):
    shapes = [jax.ShapeDtypeStruct(shape, f32) for shape in outs]
    if weights_out:
        shapes.append(jax.ShapeDtypeStruct(WEIGHTS, bf16))
    moved = sum(4 * math.prod(shape) for shape in outs) + sum(x.size * 4 for x in operands)
    places = [pl.BlockSpec(memory_space=pltpu.HBM if n < far else pltpu.VMEM) for n in range(len(operands))]
    out_places = [pl.BlockSpec(memory_space=pltpu.VMEM)] * (len(shapes) - far_outs)
    out_places += [pl.BlockSpec(memory_space=pltpu.HBM)] * far_outs
    semaphores = [pltpu.SemaphoreType.DMA((semaphores,))] if semaphores else []
    return pl.pallas_call(
        kernel,
        out_shape=tuple(shapes),
        in_specs=places,
        out_specs=tuple(out_places),
        scratch_shapes=[pltpu.VMEM(*entry) for entry in scratch] + semaphores,
        cost_estimate=pl.CostEstimate(flops=micros * 10**9, bytes_accessed=moved, transcendentals=0),
        compiler_params=pltpu.CompilerParams(vmem_limit_bytes=room << 20),
        name=name,
    )(*operands)


CORE_PAIRS = [(i, i ^ 1) for i in range(4)]
CHIP_PAIRS = [(i, i ^ 2) for i in range(4)]


def on_device(
    density, velocity, energy, species, wiener, substeps, mix_rate,
    reactants, stoich, kinetic_constants, excitation_sensitivity, heat, molar,
):
    tiles = lax.axis_size("tile")
    wide = CY + 2
    vectors = (kinetic_constants, excitation_sensitivity, heat, molar)
    tables = (reactants.T, stoich) + tuple(vector[None] for vector in vectors)
    grid = (FIELDS, CZ, SPECIES, NX)
    flow_grid, noise_grid = (CZ, 8, NX), (CZ, 16, NX)
    block = (1, CZ, CY, NX)
    fields = (species.reshape(-1, NX), density, velocity, energy, wiener.reshape(-1, NX), mix_rate, substeps)

    copies = [((2048, NX), f32), (block, f32), ((3,) + block, f32), (block, f32), ((768, NX), f32),
              (block, f32), (block, jnp.int32)]
    copies += [(table.shape, f32) for table in tables]

    rates = ((3 * REACT, 4 * CZ * NX), bf16)
    held = ((3 * CZ, FIELDS, SPECIES, NX), f32)
    low, high, bundle = call(
        pack, "pack", [(MESSAGE_ROWS, NX)] * 2 + [(BUNDLE_ROWS, NX)], copies + [((256, NX), f32), ((40, NX), f32)] + [((MESSAGE_ROWS, NX), f32)] * 2,
        2, *fields, *tables, far=13, far_outs=3, semaphores=19, room=64,
    )
    low_halo = lax.ppermute(high, "tile", [(i, i + 1) for i in range(tiles - 1)])
    high_halo = lax.ppermute(low, "tile", [(i + 1, i) for i in range(tiles - 1)])
    (
        own, flow, noise_first, noise_second, noise_sum, inner_flow, inner_total, inner_reacted, inner_matrices,
        consts, weights,
    ) = call(
        inner, "inner",
        [(CY,) + grid, (CY,) + flow_grid, (CY,) + noise_grid, (CY,) + noise_grid, (CZ, 24, NX),
         (INNER,) + flow_grid, (CZ, INNER, SPECIES, NX), (INNER,) + grid, (INNER, 256, CZ * NX), (224, NX)],
        [((INNER,) + grid, f32), ((3 * REACT, 3 * CZ * NX), bf16), held],
        8, bundle, weights_out=True,
    )
    carried, flow_one, mine, other = call(
        first_edge, "first_edge",
        [(EDGES,) + grid, (wide,) + flow_grid] + [(2, wide, SPECIES, NX)] * 2,
        [((8,) + grid, f32), ((8,) + flow_grid, f32), ((EDGES,) + noise_grid, f32), ((CZ, wide, SPECIES, NX), f32)],
        2, own, flow, noise_first, inner_flow, inner_total, low_halo, high_halo,
    )
    mine = mine + lax.ppermute(other, "field", CORE_PAIRS)
    mine, carried = lax.optimization_barrier((mine, carried))
    sum_mine = mine + lax.ppermute(mine, "field", CHIP_PAIRS)
    sum_other = lax.ppermute(sum_mine, "field", CORE_PAIRS)
    edge_matrices, partial, second = call(
        react_edge, "react_edge",
        [(EDGES, 256, CZ * NX), (CY,) + grid, (CZ, 152, NX)],
        [rates, held, ((EDGES,) + grid, f32), ((wide,) + grid, f32), ((CY,) + flow_grid, f32)],
        6, carried, flow_one, inner_reacted, noise_second, noise_sum, weights, consts,
    )
    second = second + lax.ppermute(second, "field", CORE_PAIRS)
    second_far = lax.ppermute(second, "field", CHIP_PAIRS)
    matrices_two, own_part, shared, flow_two = call(
        second_step, "second_step",
        [(CY, 256, CZ * NX), (CY,) + grid, (wide, CZ, SPECIES, NX), (CY,) + flow_grid],
        [((CZ, wide, SPECIES, NX), f32), ((wide,) + flow_grid, f32), rates, held],
        10, sum_mine, sum_other, flow_one, inner_matrices, edge_matrices, partial, noise_second, weights, consts,
    )
    flow_out, species_out = call(
        finish, "finish",
        [(5, CZ, CY, NX), (FIELDS * SPECIES, CZ, CY, NX)],
        [((CZ, 152, NX), f32), held, ((CZ, FIELDS * SPECIES, CY, NX), f32)],
        4, second, second_far, shared, flow_two, matrices_two, own_part, consts,
        far_outs=1, semaphores=CZ,
    )
    return flow_out[:, None], species_out.reshape(species.shape)


def solution(mesh):
    placed = (
        P("tile", None, None, None),
        P(None, "tile", None, None, None),
        P("tile", None, None, None),
        P("field", None, "tile", None, None, None),
        P(None, "field", None, "tile", None, None, None),
        P("tile", None, None, None),
        P("tile", None, None, None),
        P(),
        P(),
        P(),
        P(),
        P(),
        P(),
    )
    return jax.shard_map(
        on_device,
        mesh=mesh,
        in_specs=placed,
        out_specs=(P(None, "tile", None, None, None), P("field", None, "tile", None, None, None)),
        check_vma=False,
    )
```
